512 devices in a mesh: blk: 64 (over y, x, z_lo), freq: 8 (over z_hi, core).
Axes of the slice: x: 4, y: 8, z: 8 (z_hi: 4, z_lo: 2; z = z_hi * 2 + z_lo), core: 2. Of those that a mesh axis runs over, the one named last changes fastest.
Arguments:
- recorded: bfloat16 [8, 2, 1024, 16384], P('freq', None, 'blk'), may hold values from -6 to 6
- mirror: bfloat16 [8, 2, 192, 16384], P('freq', None, None, 'blk')
- live_counts: int32 [8, 64], P('freq', 'blk'), may hold values from 64 to 256, as said below
- bins: int32 [8, 1024, 2], P('freq', 'blk'), may hold values from 0 to 127, as said below
- bin_weight: float32 [8, 1024, 2], P('freq', 'blk'), may hold values from 0.25 to 1
- taper_lo: int32 [8, 1024], P('freq', 'blk'), may hold values from 0 to 47
- taper_hi: int32 [8, 1024], P('freq', 'blk'), may hold values from 144 to 192
- gain: float32 [8], P('freq'), as said below
Outputs:
- predicted: float32 [8, 2, 128, 192], P('freq', None, 'blk')
The draws below stay inside these ranges and needn't reach their ends.
Inputs may be any that keep to these rules, and one draw needn't show every extreme that they name: `live_counts`: in each frequency slice one block is fully live. The two bins of a trace differ. Among the 32 entries of the traces of one device, no bin is named more than 2 times; one bin is named exactly 2 times by the traces of every device. `gain`: Positive.
All inputs are finite; a program needn't handle non-finite values.
Results may differ from the reference program's by a relative error of at most 0.0003.
Values may be sent and summed in bfloat16 or wider, within the bound.
A program may use at most 64 MiB of HBM per device.

```python
import math
import jax
import jax.numpy as jnp
from jax import lax

SURF = 16384
SURF_DEV = 256
R_DEV = 16
RECV = 1024
SRC = 192
FREQS = 8
MOST = 2
BINS = 128
RAMP = 24
N_BLK = 64


def draw_mirror(key, part):
    key_scale, key_base = jax.random.split(key)
    spread = math.log(10.0)
    base = jax.random.normal(key_base, (FREQS, 2, SRC, SURF), jnp.float32)
    scales = jnp.exp(jax.random.uniform(key_scale, (SRC,), jnp.float32) * spread)
    factor = 1.0 / (4.6 * math.sqrt(2.0 * SURF))
    return (base * scales[None, None, :, None] * factor).astype(jnp.bfloat16)


def draw_gain(key, part):
    position = jnp.arange(FREQS, dtype=jnp.int32).astype(jnp.float32) / max(FREQS - 1, 1)
    jitter = jax.random.uniform(key, (FREQS,), jnp.float32, 0.8, 1.25)
    return (jnp.power(10.0, position) * jitter).astype(jnp.float32)


def draw_live_counts(key, part):
    key_count, key_full = jax.random.split(jax.random.fold_in(key, 11))
    lowest = max(1, SURF_DEV // 4)
    counts = jax.random.randint(key_count, (FREQS, N_BLK), lowest, SURF_DEV + 1, dtype=jnp.int32)
    full = jax.random.randint(key_full, (FREQS,), 0, N_BLK, dtype=jnp.int32)
    column = jnp.arange(N_BLK, dtype=jnp.int32)
    return jnp.where(column[None, :] == full[:, None], SURF_DEV, counts).astype(jnp.int32)


def draw_bins(key, part):
    key_star, key_run, key_perm = jax.random.split(jax.random.fold_in(key, 23), 3)
    star = jax.random.randint(key_star, (), 0, BINS, dtype=jnp.int32)
    entries = 2 * R_DEV
    blocks = FREQS * N_BLK
    position = jnp.arange(entries, dtype=jnp.int32)

    def one_block(index):
        spans = jax.random.randint(jax.random.fold_in(key_run, index), (entries,), 1, MOST + 1, dtype=jnp.int32)
        spans = spans.at[0].set(MOST)
        starts = jnp.cumsum(spans) - spans
        run_id = jnp.sum((starts[None, :] <= position[:, None]).astype(jnp.int32), axis=1) - 1
        order = jax.random.permutation(jax.random.fold_in(key_perm, index), BINS).astype(jnp.int32)
        order = jnp.where(order == star, order[0], order)
        order = order.at[0].set(star)
        picked = order[run_id]
        return picked.reshape(2, R_DEV).T
    table = jax.vmap(one_block)(jnp.arange(blocks, dtype=jnp.int32))
    return table.reshape(FREQS, N_BLK * R_DEV, 2).astype(jnp.int32)


def place_ends(drawn, rng, least, largest):
    extent = drawn.shape
    index_at = [jax.random.randint(jax.random.fold_in(rng, axis), (), 0, extent[axis]) for axis in range(len(extent))]
    drawn = drawn.at[tuple(index_at)].set(least)
    longest = extent.index(max(extent))
    index_at[longest] = (index_at[longest] + 1) % extent[longest]
    return drawn.at[tuple(index_at)].set(largest)


def level_of(key, extent, cuts, smallest, high):
    def one(dim, parts):
        steps = jax.random.uniform(jax.random.fold_in(jax.random.fold_in(key, 6), dim), (parts,), jnp.float32, smallest / len(cuts), high / len(cuts))
        return jnp.repeat(jnp.exp(steps), extent[dim] // parts).reshape((-1,) + (1,) * (len(extent) - dim - 1))

    level = one(*cuts[0])
    for cut in cuts[1:]:
        level = level * one(*cut)
    return level


def bell_draw(stream_key, extent, scale, most, shards=(), kind=jnp.bfloat16):
    loudness = level_of(stream_key, extent, shards, -0.22, 0.18) if shards else 1.0
    values = jax.random.normal(stream_key, extent, jnp.float32) * scale * loudness
    return jnp.minimum(jnp.maximum(values, -most), most).astype(kind)


def setup_inputs(seed: int = 0) -> dict:
    seeds = jax.random.split(jax.random.key(seed), 9)
    recorded = bell_draw(seeds[0], (FREQS, 2, RECV, SURF), 1.0, 6.0, ((0, 8), (2, 64)))
    mirror = draw_mirror(jax.random.fold_in(seeds[8], 71), 0)
    live_counts = draw_live_counts(jax.random.fold_in(seeds[8], 71), 0)
    bins = draw_bins(jax.random.fold_in(seeds[8], 71), 0)
    bin_weight = jnp.clip(0.25 + 0.75 * jax.random.uniform(seeds[4], (FREQS, RECV, 2), jnp.float32) ** level_of(seeds[4], (FREQS, RECV, 2), ((0, 8), (1, 64)), -0.2, 0.2), 0.25, 1.0)
    taper_lo = place_ends(jax.random.randint(seeds[5], (FREQS, RECV), 0, SRC // 4), jax.random.fold_in(seeds[5], 1), 0, (SRC // 4) - 1).astype(jnp.int32)
    taper_hi = place_ends(jax.random.randint(seeds[6], (FREQS, RECV), 3 * SRC // 4, SRC + 1), jax.random.fold_in(seeds[6], 1), 3 * SRC // 4, SRC).astype(jnp.int32)
    gain = draw_gain(jax.random.fold_in(seeds[8], 71), 0)
    return dict(recorded=recorded, mirror=mirror, live_counts=live_counts, bins=bins, bin_weight=bin_weight, taper_lo=taper_lo, taper_hi=taper_hi, gain=gain)


def taper_weights(lo_col, hi_col, count):
    column = jnp.arange(count, dtype=jnp.int32).astype(jnp.float32)[None, :]
    rise = jnp.clip((column - lo_col.astype(jnp.float32)[:, None] + 1.0) / RAMP, 0.0, 1.0)
    fall = jnp.clip((hi_col.astype(jnp.float32)[:, None] - column) / RAMP, 0.0, 1.0)
    return rise * fall

def reference(recorded, mirror, live_counts, bins, bin_weight, taper_lo, taper_hi, gain):
    point = jnp.arange(SURF, dtype=jnp.int32)
    block = point // SURF_DEV
    offset = point % SURF_DEV
    bin_ids = jnp.arange(BINS, dtype=jnp.int32)

    def one_slice(index):
        counts = live_counts[index]
        live = (offset < counts[block]).astype(jnp.float32)
        left = recorded[index].astype(jnp.float32)
        right = mirror[index].astype(jnp.float32) * live[None, None, :]
        prod = jnp.einsum('ark,bsk->arbs', left, right, precision=lax.Precision.HIGHEST)
        real_part = prod[0, :, 0] - prod[1, :, 1]
        imag_part = prod[0, :, 1] + prod[1, :, 0]
        taper = taper_weights(taper_lo[index], taper_hi[index], SRC)
        weights = bin_weight[index]
        lists = bins[index]
        mapping = jnp.zeros((BINS, RECV), jnp.float32)
        for which in range(2):
            mapping = mapping + jnp.where(lists[:, which][None, :] == bin_ids[:, None], weights[:, which][None, :], 0.0)
        values = jnp.stack([real_part * taper, imag_part * taper], axis=0)
        binned = jnp.einsum('br,crs->cbs', mapping, values, precision=lax.Precision.HIGHEST)
        return binned * gain[index]
    scaled = lax.map(one_slice, jnp.arange(FREQS, dtype=jnp.int32))
    energy = lax.optimization_barrier(jnp.sum(scaled * scaled, axis=(0, 1, 3)))
    norm = jnp.sqrt(energy / (FREQS * 2 * SRC) + 1e-06)
    return scaled / norm[None, None, :, None]
```

```python
import jax
import jax.numpy as jnp
from jax import lax
from jax.experimental import pallas as pl
from jax.experimental.pallas import tpu as pltpu
from jax.sharding import PartitionSpec as P

RAMP = 24
NY, NX, NZ = 8, 4, 2
MESH = pl.DeviceIdType.MESH
F32 = jnp.float32
NT = (((1,), (1,)), ((), ()))
NN = (((1,), (0,)), ((), ()))


def make_kernel(n_freq, r_dev, src, k_dev):
    n_plane = NX * NZ
    rows = n_plane * r_dev
    n_bins = 2 * NY * n_plane
    half = NY // 2
    tail = src - 128

    def kernel(rec, mir, live_hbm, bins_hbm, wts_hbm, lo_hbm, hi_hbm, gain_hbm, out,
               live, bins, wts, lo, hi, gain, raw, sbuf, rbuf, meta, mapt, tap, acc, asend, abuf, bsend, bbuf, esend, ebuf,
               l_sem, p_sem, s_send, s_recv, r_send, r_recv, m_send, m_recv,
               a_send, a_recv, b_send, b_recv, e_send, e_recv):
        blk = lax.axis_index("blk")
        frq = lax.axis_index("freq")
        y = blk // n_plane
        p = blk % n_plane
        x = p // NZ
        z = p % NZ

        load = pltpu.make_async_copy(mir.at[0], raw, l_sem)
        load.start()
        small = [(live_hbm, live), (bins_hbm, bins), (wts_hbm, wts), (lo_hbm, lo), (hi_hbm, hi), (gain_hbm, gain)]
        small = [pltpu.make_async_copy(a, b, p_sem.at[i]) for i, (a, b) in enumerate(small)]
        for copy in small:
            copy.start()

        offsets = [(dx, dz) for dx in range(NX) for dz in range(NZ) if dx or dz]

        def plane_of(dx, dz):
            return ((x + dx) % NX) * NZ + (z + dz) % NZ

        peers = [plane_of(dx, dz) for dx, dz in offsets]
        y_of = [(y + d) % NY for d in range(NY)]
        f_of = [(frq + d) % n_freq for d in range(n_freq)]

        barrier = pltpu.get_barrier_semaphore()
        for q in peers:
            pl.semaphore_signal(barrier, inc=1, device_id=(y * n_plane + q, frq), device_id_type=MESH)
        for d in range(1, NY):
            pl.semaphore_signal(barrier, inc=1, device_id=(y_of[d] * n_plane + p, frq), device_id_type=MESH)
        for d in range(1, n_freq):
            pl.semaphore_signal(barrier, inc=1, device_id=(blk, f_of[d]), device_id_type=MESH)

        for copy in small:
            copy.wait()

        def column(line):
            line = jnp.broadcast_to(line.astype(F32), (r_dev, r_dev))
            on = lax.broadcasted_iota(jnp.int32, (r_dev, r_dev), 0) == lax.broadcasted_iota(jnp.int32, (r_dev, r_dev), 1)
            return jnp.sum(jnp.where(on, line, 0.0), axis=1, keepdims=True)

        lane = lax.broadcasted_iota(jnp.int32, (r_dev, 128), 1)
        table = jnp.zeros((r_dev, 128), F32)
        for i, line in enumerate([bins[0:1], bins[1:2], wts[0:1], wts[1:2], lo[...], hi[...]]):
            table = jnp.where(lane == i, column(line), table)
        mine = pl.ds(pl.multiple_of(p * r_dev, r_dev), r_dev)
        meta[mine, :] = table

        load.wait()
        on = lax.broadcasted_iota(jnp.int32, (src, k_dev), 1) < live[...]
        for c in range(2):
            sbuf[y, c] = jnp.where(on, raw[c], jnp.zeros_like(raw[c]))

        pl.semaphore_wait(barrier, len(peers) + NY - 1 + n_freq - 1)

        def ring(way, step, c):
            owner = (y - step) % NY if way == 0 else (y + step) % NY
            to = y_of[1] if way == 0 else y_of[NY - 1]
            i = step * 2 + c
            return pltpu.make_async_remote_copy(
                src_ref=sbuf.at[owner, c], dst_ref=sbuf.at[owner, c],
                send_sem=s_send.at[way, i], recv_sem=s_recv.at[way, i],
                device_id=(to * n_plane + p, frq), device_id_type=MESH)

        def landed(way, step, c):
            owner = (y - step - 1) % NY if way == 0 else (y + step + 1) % NY
            i = step * 2 + c
            pltpu.make_async_remote_copy(
                src_ref=sbuf.at[owner, c], dst_ref=sbuf.at[owner, c],
                send_sem=s_send.at[way, i], recv_sem=s_recv.at[way, i],
                device_id=(y_of[1] * n_plane + p, frq), device_id_type=MESH).wait_recv()

        for c in range(2):
            for way in range(2):
                ring(way, 0, c if way == 0 else 1 - c).start()

        def send_rows(d, carry):
            yy = (y + d) % NY
            at = (yy * n_plane) * k_dev
            for i, q in enumerate(peers):
                cols = pl.ds(pl.multiple_of(at + q * k_dev, k_dev), k_dev)
                pltpu.make_async_remote_copy(
                    src_ref=rec.at[0, :, :, cols], dst_ref=rbuf.at[yy, :, mine, :],
                    send_sem=r_send, recv_sem=r_recv.at[yy],
                    device_id=(y * n_plane + q, frq), device_id_type=MESH).start()
            cols = pl.ds(pl.multiple_of(at + p * k_dev, k_dev), k_dev)
            pltpu.make_async_copy(rec.at[0, :, :, cols], rbuf.at[yy, :, mine, :], r_recv.at[yy]).start()
            return carry

        lax.fori_loop(0, NY, send_rows, 0)

        def meta_copy(i):
            return pltpu.make_async_remote_copy(
                src_ref=meta.at[mine, :], dst_ref=meta.at[mine, :],
                send_sem=m_send.at[i], recv_sem=m_recv.at[i],
                device_id=(y * n_plane + peers[i], frq), device_id_type=MESH)

        for i in range(len(peers)):
            meta_copy(i).start()

        def pass_on(step):
            for c in range(2):
                for way in range(2):
                    part = c if way == 0 else 1 - c
                    if step + 1 < half or c == 0:
                        landed(way, step, part)
                    if step + 1 < half - 1 or (step + 1 == half - 1 and c == 0):
                        ring(way, step + 1, part).start()

        def from_peer(i):
            dx, dz = offsets[i]
            q = plane_of(-dx, -dz)
            rows_q = pl.ds(pl.multiple_of(q * r_dev, r_dev), r_dev)
            pltpu.make_async_remote_copy(
                src_ref=meta.at[rows_q, :], dst_ref=meta.at[rows_q, :],
                send_sem=m_send.at[i], recv_sem=m_recv.at[i],
                device_id=(y * n_plane + peers[i], frq), device_id_type=MESH).wait_recv()

        pass_on(0)
        for i in range(len(peers)):
            from_peer(i)
        info = meta[...]
        place = lax.broadcasted_iota(jnp.int32, (rows, n_bins), 1)
        per = 2 * NY
        named = (place % per // 2) * (2 * n_plane) + (place // per) * 2 + place % 2
        named = named.astype(F32)
        spread = jnp.where(info[:, 0:1] == named, info[:, 2:3], 0.0) + jnp.where(info[:, 1:2] == named, info[:, 3:4], 0.0)
        mapt[...] = spread.T
        at = lax.broadcasted_iota(jnp.int32, (rows, src), 1).astype(F32)
        rise = jnp.clip((at - info[:, 4:5] + 1.0) / RAMP, 0.0, 1.0)
        fall = jnp.clip((info[:, 5:6] - at) / RAMP, 0.0, 1.0)
        tap[...] = rise * fall
        for step in range(1, half - 1):
            pass_on(step)

        def product(d, first=False):
            yy = y_of[d % NY]
            left = rbuf[yy].reshape(2 * rows, k_dev)
            for c in range(2):
                part = lax.dot_general(left, sbuf[yy, c], NT, preferred_element_type=F32)
                if first:
                    acc[c] = part
                else:
                    acc[c] += part

        def rows_landed(d):
            yy = y_of[d % NY]
            pltpu.make_async_copy(rbuf.at[yy], rbuf.at[yy], r_recv.at[yy]).wait()

        for i, d in enumerate([0] + [s * k for k in range(1, half) for s in (1, -1)]):
            rows_landed(d)
            product(d, first=i == 0)
        rows_landed(half)
        pass_on(half - 1)
        product(half)

        binned = []
        for c in range(2):
            if c == 0:
                value = acc[0, 0:rows] - acc[1, rows:2 * rows]
            else:
                value = acc[1, 0:rows] + acc[0, rows:2 * rows]
            binned.append(lax.dot_general(mapt[...], value * tap[...], NN, precision=lax.Precision.HIGHEST, preferred_element_type=F32))
        asend[:, 0:128] = binned[0][:, 0:128]
        asend[:, 128:256] = binned[1][:, 0:128]
        asend[:, 256:256 + tail] = binned[0][:, 128:src]
        asend[:, 256 + tail:256 + 2 * tail] = binned[1][:, 128:src]

        def a_copy(i):
            to = pl.ds(pl.multiple_of(peers[i] * per, per), per)
            return pltpu.make_async_remote_copy(
                src_ref=asend.at[to, :], dst_ref=abuf.at[i],
                send_sem=a_send.at[i], recv_sem=a_recv.at[i],
                device_id=(y * n_plane + peers[i], frq), device_id_type=MESH)

        for i in range(len(peers)):
            a_copy(i).start()
        total = asend[pl.ds(pl.multiple_of(p * per, per), per), :]
        for i in range(len(peers)):
            a_copy(i).wait_recv()
            total = total + abuf[i]

        bsend[...] = jnp.zeros_like(bsend)
        for d in range(NY):
            for k in range(3):
                bsend[d, 2 * k:2 * k + 2, :] = total[2 * d:2 * d + 2, 128 * k:128 * k + 128]

        def b_copy(d):
            return pltpu.make_async_remote_copy(
                src_ref=bsend.at[y_of[d]], dst_ref=bbuf.at[d - 1],
                send_sem=b_send.at[d - 1], recv_sem=b_recv.at[d - 1],
                device_id=(y_of[d] * n_plane + p, frq), device_id_type=MESH)

        for d in range(1, NY):
            b_copy(d).start()
        tile = bsend[y]
        for d in range(1, NY):
            b_copy(d).wait_recv()
            tile = tile + bbuf[d - 1]
        scaled = tile * gain[...]
        square = scaled * scaled
        esend[...] = square

        def e_copy(d):
            return pltpu.make_async_remote_copy(
                src_ref=esend, dst_ref=ebuf.at[d - 1],
                send_sem=e_send.at[d - 1], recv_sem=e_recv.at[d - 1],
                device_id=(blk, f_of[d]), device_id_type=MESH)

        for d in range(1, n_freq):
            e_copy(d).start()
        for way in range(2):
            for step in range(half):
                for c in range(2):
                    part = c if way == 0 else 1 - c
                    if step < half - 1 or c == 0:
                        ring(way, step, part).wait_send()
        pltpu.make_async_copy(rbuf.at[:, :, pl.ds(0, rows - r_dev), :], rbuf.at[:, :, pl.ds(0, rows - r_dev), :], r_send).wait()
        for i in range(len(peers)):
            meta_copy(i).wait_send()
            a_copy(i).wait_send()
        for d in range(1, NY):
            b_copy(d).wait_send()
        for d in range(1, n_freq):
            e_copy(d).wait_recv()
            square = square + ebuf[d - 1]
        for d in range(1, n_freq):
            e_copy(d).wait_send()
        energy = jnp.sum(square[0:2] + square[2:4] + square[4:6], axis=1, keepdims=True)
        norm = jnp.sqrt(energy / (n_freq * 2 * src) + 1e-06)
        for c in range(2):
            out[0, c, :, 0:128] = scaled[2 * c:2 * c + 2] / norm
            out[0, c, :, 128:src] = scaled[4:6, c * tail:(c + 1) * tail] / norm

    return kernel


def solution(mesh):
    n_freq = mesh.shape["freq"]

    def local(recorded, mirror, live_counts, bins, bin_weight, taper_lo, taper_hi, gain):
        r_dev = recorded.shape[2]
        src, k_dev = mirror.shape[2], mirror.shape[3]
        n_plane = NX * NZ
        rows, per, n_peer, half = n_plane * r_dev, 2 * NY, n_plane - 1, NY // 2
        hbm, vmem = (pl.BlockSpec(memory_space=m) for m in (pltpu.HBM, pltpu.VMEM))
        dma = pltpu.SemaphoreType.DMA
        bf16 = jnp.bfloat16
        return pl.pallas_call(
            make_kernel(n_freq, r_dev, src, k_dev),
            out_shape=jax.ShapeDtypeStruct((1, 2, 2, src), F32),
            in_specs=[hbm] * 8,
            out_specs=vmem,
            scratch_shapes=[
                pltpu.VMEM((1, 1), jnp.int32),
                pltpu.VMEM((2, r_dev), jnp.int32),
                pltpu.VMEM((2, r_dev), F32),
                pltpu.VMEM((1, r_dev), jnp.int32),
                pltpu.VMEM((1, r_dev), jnp.int32),
                pltpu.VMEM((1, 1), F32),
                pltpu.VMEM((2, src, k_dev), bf16),
                pltpu.VMEM((NY, 2, src, k_dev), bf16),
                pltpu.VMEM((NY, 2, rows, k_dev), bf16),
                pltpu.VMEM((rows, 128), F32),
                pltpu.VMEM((2 * NY * n_plane, rows), F32),
                pltpu.VMEM((rows, src), F32),
                pltpu.VMEM((2, 2 * rows, src), F32),
                pltpu.VMEM((per * n_plane, 2 * src), F32),
                pltpu.VMEM((n_peer, per, 2 * src), F32),
                pltpu.VMEM((NY, 8, 128), F32),
                pltpu.VMEM((NY - 1, 8, 128), F32),
                pltpu.VMEM((8, 128), F32),
                pltpu.VMEM((n_freq - 1, 8, 128), F32),
                dma, dma((6,)),
                dma((2, 2 * half)), dma((2, 2 * half)),
                dma, dma((NY,)),
                dma((n_peer,)), dma((n_peer,)),
                dma((n_peer,)), dma((n_peer,)),
                dma((NY - 1,)), dma((NY - 1,)),
                dma((n_freq - 1,)), dma((n_freq - 1,)),
            ],
            compiler_params=pltpu.CompilerParams(
                collective_id=0, has_side_effects=True, vmem_limit_bytes=63 * 1024 * 1024
            ),
        )(recorded, mirror, live_counts, bins[0].T, bin_weight[0].T, taper_lo, taper_hi, gain.reshape(1, 1))

    in_specs = (
        P("freq", None, "blk", None),
        P("freq", None, None, "blk"),
        P("freq", "blk"),
        P("freq", "blk", None),
        P("freq", "blk", None),
        P("freq", "blk"),
        P("freq", "blk"),
        P("freq"),
    )
    out_specs = P("freq", None, "blk", None)
    return jax.shard_map(local, mesh=mesh, in_specs=in_specs, out_specs=out_specs, check_vma=False)
```

```python
import jax
import jax.numpy as jnp
from jax import lax
from jax.experimental import pallas as pl
from jax.experimental.pallas import tpu as pltpu
from jax.sharding import PartitionSpec as P

RAMP = 24
NY, NX, NZ, NC = 8, 4, 2, 2
MESH = pl.DeviceIdType.MESH
F32 = jnp.float32
NT = (((1,), (1,)), ((), ()))
NN = (((1,), (0,)), ((), ()))


def make_kernel(n_freq, r_dev, src, k_dev):
    n_plane = NX * NZ
    rows = n_plane * r_dev
    n_bins = 2 * NY * n_plane
    half = NY // 2
    tail = src - 128

    def kernel(rec, mir, live_hbm, bins_hbm, wts_hbm, lo_hbm, hi_hbm, gain_hbm, out,
               live, bins, wts, lo, hi, gain, raw, sbuf, rbuf, meta, mapt, tap, acc, asend, abuf, bsend, bbuf, esend, ebuf,
               l_sem, p_sem, word, s_send, s_recv, r_send, r_recv, m_send, m_recv,
               a_send, a_recv, b_send, b_recv, e_send, e_recv):
        blk = lax.axis_index("blk")
        frq = lax.axis_index("freq")
        y = blk // n_plane
        p = blk % n_plane
        x = p // NZ
        z = p % NZ

        core = frq % NC
        deep = (frq // NC) * NZ + z
        nz = (n_freq // NC) * NZ

        offsets = [(dx, dz) for dx in range(NX) for dz in range(NZ) if dx or dz]

        def plane_of(dx, dz):
            return ((x + dx) % NX) * NZ + (z + dz) % NZ

        peers = [plane_of(dx, dz) for dx, dz in offsets]
        y_of = [(y + d) % NY for d in range(NY)]
        f_of = [(frq + d) % n_freq for d in range(n_freq)]

        near_y = [(y_of[d] * n_plane + p, frq) for d in sorted({1, NY - 1})]
        near = []
        for d in sorted({1 % NX, NX - 1} - {0}):
            near.append((y * n_plane + ((x + d) % NX) * NZ + z, frq))
        for d in sorted({1 % nz, nz - 1} - {0}):
            at = (deep + d) % nz
            near.append((y * n_plane + x * NZ + at % NZ, (at // NZ) * NC + core))
        if NC == 2:
            near.append((blk, frq - core + 1 - core))

        barrier = pltpu.get_barrier_semaphore()
        for to in near_y + near:
            pl.semaphore_signal(barrier, inc=1, device_id=to, device_id_type=MESH)

        loads = [pltpu.make_async_copy(mir.at[0, c], raw.at[c], l_sem.at[c]) for c in range(2)]
        small = [(live_hbm, live), (bins_hbm, bins), (wts_hbm, wts), (lo_hbm, lo), (hi_hbm, hi), (gain_hbm, gain)]
        small = [pltpu.make_async_copy(a, b, p_sem.at[i]) for i, (a, b) in enumerate(small)]
        small[0].start()
        for copy in loads + small[1:]:
            copy.start()

        small[0].wait()
        on = lax.broadcasted_iota(jnp.int32, (src, k_dev), 1) < live[...]
        for c in range(2):
            loads[c].wait()
            sbuf[y, c] = jnp.where(on, raw[c], jnp.zeros_like(raw[c]))

        pl.semaphore_wait(barrier, len(near_y) + len(near))

        def ring(way, step, c):
            owner = (y - step) % NY if way == 0 else (y + step) % NY
            to = y_of[1] if way == 0 else y_of[NY - 1]
            i = step * 2 + c
            return pltpu.make_async_remote_copy(
                src_ref=sbuf.at[owner, c], dst_ref=sbuf.at[owner, c],
                send_sem=s_send.at[way, i], recv_sem=s_recv.at[way, i],
                device_id=(to * n_plane + p, frq), device_id_type=MESH)

        def landed(way, step, c):
            owner = (y - step - 1) % NY if way == 0 else (y + step + 1) % NY
            i = step * 2 + c
            pltpu.make_async_remote_copy(
                src_ref=sbuf.at[owner, c], dst_ref=sbuf.at[owner, c],
                send_sem=s_send.at[way, i], recv_sem=s_recv.at[way, i],
                device_id=(y_of[1] * n_plane + p, frq), device_id_type=MESH).wait_recv()

        for c in range(2):
            for way in range(2):
                ring(way, 0, c if way == 0 else 1 - c).start()

        def tell(i):
            for to in near:
                pl.semaphore_signal(word.at[i], inc=1, device_id=to, device_id_type=MESH)

        def heard(i):
            pl.semaphore_wait(word.at[i], len(near))

        tell(0)

        for copy in small[1:]:
            copy.wait()

        def column(line):
            line = jnp.broadcast_to(line.astype(F32), (r_dev, r_dev))
            on = lax.broadcasted_iota(jnp.int32, (r_dev, r_dev), 0) == lax.broadcasted_iota(jnp.int32, (r_dev, r_dev), 1)
            return jnp.sum(jnp.where(on, line, 0.0), axis=1, keepdims=True)

        lane = lax.broadcasted_iota(jnp.int32, (r_dev, 128), 1)
        table = jnp.zeros((r_dev, 128), F32)
        for i, line in enumerate([bins[0:1], bins[1:2], wts[0:1], wts[1:2], lo[...], hi[...]]):
            table = jnp.where(lane == i, column(line), table)
        mine = pl.ds(pl.multiple_of(p * r_dev, r_dev), r_dev)
        meta[mine, :] = table

        heard(0)
        tell(1)
        heard(1)
        tell(2)

        def send_rows(d, carry):
            yy = (y + d) % NY
            at = (yy * n_plane) * k_dev
            for i, q in enumerate(peers):
                cols = pl.ds(pl.multiple_of(at + q * k_dev, k_dev), k_dev)
                pltpu.make_async_remote_copy(
                    src_ref=rec.at[0, :, :, cols], dst_ref=rbuf.at[yy, :, mine, :],
                    send_sem=r_send, recv_sem=r_recv.at[yy],
                    device_id=(y * n_plane + q, frq), device_id_type=MESH).start()
            cols = pl.ds(pl.multiple_of(at + p * k_dev, k_dev), k_dev)
            pltpu.make_async_copy(rec.at[0, :, :, cols], rbuf.at[yy, :, mine, :], r_recv.at[yy]).start()
            return carry

        def send_part(i):
            ends = [0, 3, 6, NY] if half == 4 else [0, NY]
            if i < len(ends) - 1:
                lax.fori_loop(ends[i], ends[i + 1], send_rows, 0)

        send_part(0)

        def meta_copy(i):
            return pltpu.make_async_remote_copy(
                src_ref=meta.at[mine, :], dst_ref=meta.at[mine, :],
                send_sem=m_send.at[i], recv_sem=m_recv.at[i],
                device_id=(y * n_plane + peers[i], frq), device_id_type=MESH)

        for i in range(len(peers)):
            meta_copy(i).start()

        def pass_on(step):
            for c in range(2):
                for way in range(2):
                    part = c if way == 0 else 1 - c
                    if step + 1 < half or c == 0:
                        landed(way, step, part)
                    if step + 1 < half - 1 or (step + 1 == half - 1 and c == 0):
                        ring(way, step + 1, part).start()
                if c == 0:
                    send_part(step + 1)

        def from_peer(i):
            dx, dz = offsets[i]
            q = plane_of(-dx, -dz)
            rows_q = pl.ds(pl.multiple_of(q * r_dev, r_dev), r_dev)
            pltpu.make_async_remote_copy(
                src_ref=meta.at[rows_q, :], dst_ref=meta.at[rows_q, :],
                send_sem=m_send.at[i], recv_sem=m_recv.at[i],
                device_id=(y * n_plane + peers[i], frq), device_id_type=MESH).wait_recv()

        pass_on(0)
        heard(2)
        tell(3)
        for i in range(len(peers)):
            from_peer(i)
        info = meta[...]
        place = lax.broadcasted_iota(jnp.int32, (rows, n_bins), 1)
        per = 2 * NY
        named = (place % per // 2) * (2 * n_plane) + (place // per) * 2 + place % 2
        named = named.astype(F32)
        spread = jnp.where(info[:, 0:1] == named, info[:, 2:3], 0.0) + jnp.where(info[:, 1:2] == named, info[:, 3:4], 0.0)
        mapt[...] = spread.T
        at = lax.broadcasted_iota(jnp.int32, (rows, src), 1).astype(F32)
        rise = jnp.clip((at - info[:, 4:5] + 1.0) / RAMP, 0.0, 1.0)
        fall = jnp.clip((info[:, 5:6] - at) / RAMP, 0.0, 1.0)
        tap[...] = rise * fall
        for step in range(1, half - 1):
            pass_on(step)
        heard(3)

        def product(d, first=False):
            yy = y_of[d % NY]
            left = rbuf[yy].reshape(2 * rows, k_dev)
            for c in range(2):
                part = lax.dot_general(left, sbuf[yy, c], NT, preferred_element_type=F32)
                if first:
                    acc[c] = part
                else:
                    acc[c] += part

        def rows_landed(d):
            yy = y_of[d % NY]
            pltpu.make_async_copy(rbuf.at[yy], rbuf.at[yy], r_recv.at[yy]).wait()

        for i, d in enumerate([0] + [s * k for k in range(1, half) for s in (1, -1)]):
            rows_landed(d)
            product(d, first=i == 0)
        rows_landed(half)
        pass_on(half - 1)
        product(half)

        binned = []
        for c in range(2):
            if c == 0:
                value = acc[0, 0:rows] - acc[1, rows:2 * rows]
            else:
                value = acc[1, 0:rows] + acc[0, rows:2 * rows]
            binned.append(lax.dot_general(mapt[...], value * tap[...], NN, precision=lax.Precision.HIGHEST, preferred_element_type=F32))
        asend[:, 0:128] = binned[0][:, 0:128]
        asend[:, 128:256] = binned[1][:, 0:128]
        asend[:, 256:256 + tail] = binned[0][:, 128:src]
        asend[:, 256 + tail:256 + 2 * tail] = binned[1][:, 128:src]

        def a_copy(i):
            to = pl.ds(pl.multiple_of(peers[i] * per, per), per)
            return pltpu.make_async_remote_copy(
                src_ref=asend.at[to, :], dst_ref=abuf.at[i],
                send_sem=a_send.at[i], recv_sem=a_recv.at[i],
                device_id=(y * n_plane + peers[i], frq), device_id_type=MESH)

        for i in range(len(peers)):
            a_copy(i).start()
        total = asend[pl.ds(pl.multiple_of(p * per, per), per), :]
        for i in range(len(peers)):
            a_copy(i).wait_recv()
            total = total + abuf[i]

        bsend[...] = jnp.zeros_like(bsend)
        for d in range(NY):
            for k in range(3):
                bsend[d, 2 * k:2 * k + 2, :] = total[2 * d:2 * d + 2, 128 * k:128 * k + 128]

        def b_copy(d):
            return pltpu.make_async_remote_copy(
                src_ref=bsend.at[y_of[d]], dst_ref=bbuf.at[d - 1],
                send_sem=b_send.at[d - 1], recv_sem=b_recv.at[d - 1],
                device_id=(y_of[d] * n_plane + p, frq), device_id_type=MESH)

        for d in range(1, NY):
            b_copy(d).start()
        tile = bsend[y]
        for d in range(1, NY):
            b_copy(d).wait_recv()
            tile = tile + bbuf[d - 1]
        scaled = tile * gain[...]
        square = scaled * scaled
        esend[...] = square

        def e_copy(d):
            return pltpu.make_async_remote_copy(
                src_ref=esend, dst_ref=ebuf.at[d - 1],
                send_sem=e_send.at[d - 1], recv_sem=e_recv.at[d - 1],
                device_id=(blk, f_of[d]), device_id_type=MESH)

        for d in range(1, n_freq):
            e_copy(d).start()
        for way in range(2):
            for step in range(half):
                for c in range(2):
                    part = c if way == 0 else 1 - c
                    if step < half - 1 or c == 0:
                        ring(way, step, part).wait_send()
        pltpu.make_async_copy(rbuf.at[:, :, pl.ds(0, rows - r_dev), :], rbuf.at[:, :, pl.ds(0, rows - r_dev), :], r_send).wait()
        for i in range(len(peers)):
            meta_copy(i).wait_send()
            a_copy(i).wait_send()
        for d in range(1, NY):
            b_copy(d).wait_send()
        for d in range(1, n_freq):
            e_copy(d).wait_recv()
            square = square + ebuf[d - 1]
        for d in range(1, n_freq):
            e_copy(d).wait_send()
        energy = jnp.sum(square[0:2] + square[2:4] + square[4:6], axis=1, keepdims=True)
        norm = jnp.sqrt(energy / (n_freq * 2 * src) + 1e-06)
        for c in range(2):
            out[0, c, :, 0:128] = scaled[2 * c:2 * c + 2] / norm
            out[0, c, :, 128:src] = scaled[4:6, c * tail:(c + 1) * tail] / norm

    return kernel


def solution(mesh):
    n_freq = mesh.shape["freq"]

    def local(recorded, mirror, live_counts, bins, bin_weight, taper_lo, taper_hi, gain):
        r_dev = recorded.shape[2]
        src, k_dev = mirror.shape[2], mirror.shape[3]
        n_plane = NX * NZ
        rows, per, n_peer, half = n_plane * r_dev, 2 * NY, n_plane - 1, NY // 2
        hbm, vmem = (pl.BlockSpec(memory_space=m) for m in (pltpu.HBM, pltpu.VMEM))
        dma = pltpu.SemaphoreType.DMA
        bf16 = jnp.bfloat16
        return pl.pallas_call(
            make_kernel(n_freq, r_dev, src, k_dev),
            out_shape=jax.ShapeDtypeStruct((1, 2, 2, src), F32),
            in_specs=[hbm] * 8,
            out_specs=vmem,
            scratch_shapes=[
                pltpu.VMEM((1, 1), jnp.int32),
                pltpu.VMEM((2, r_dev), jnp.int32),
                pltpu.VMEM((2, r_dev), F32),
                pltpu.VMEM((1, r_dev), jnp.int32),
                pltpu.VMEM((1, r_dev), jnp.int32),
                pltpu.VMEM((1, 1), F32),
                pltpu.VMEM((2, src, k_dev), bf16),
                pltpu.VMEM((NY, 2, src, k_dev), bf16),
                pltpu.VMEM((NY, 2, rows, k_dev), bf16),
                pltpu.VMEM((rows, 128), F32),
                pltpu.VMEM((2 * NY * n_plane, rows), F32),
                pltpu.VMEM((rows, src), F32),
                pltpu.VMEM((2, 2 * rows, src), F32),
                pltpu.VMEM((per * n_plane, 2 * src), F32),
                pltpu.VMEM((n_peer, per, 2 * src), F32),
                pltpu.VMEM((NY, 8, 128), F32),
                pltpu.VMEM((NY - 1, 8, 128), F32),
                pltpu.VMEM((8, 128), F32),
                pltpu.VMEM((n_freq - 1, 8, 128), F32),
                dma((2,)), dma((6,)), pltpu.SemaphoreType.REGULAR((4,)),
                dma((2, 2 * half)), dma((2, 2 * half)),
                dma, dma((NY,)),
                dma((n_peer,)), dma((n_peer,)),
                dma((n_peer,)), dma((n_peer,)),
                dma((NY - 1,)), dma((NY - 1,)),
                dma((n_freq - 1,)), dma((n_freq - 1,)),
            ],
            compiler_params=pltpu.CompilerParams(
                collective_id=0, has_side_effects=True, vmem_limit_bytes=63 * 1024 * 1024
            ),
        )(recorded, mirror, live_counts, bins[0].T, bin_weight[0].T, taper_lo, taper_hi, gain.reshape(1, 1))

    in_specs = (
        P("freq", None, "blk", None),
        P("freq", None, None, "blk"),
        P("freq", "blk"),
        P("freq", "blk", None),
        P("freq", "blk", None),
        P("freq", "blk"),
        P("freq", "blk"),
        P("freq"),
    )
    out_specs = P("freq", None, "blk", None)
    return jax.shard_map(local, mesh=mesh, in_specs=in_specs, out_specs=out_specs, check_vma=False)
```

```python
import jax
import jax.numpy as jnp
from jax import lax
from jax.experimental import pallas as pl
from jax.experimental.pallas import tpu as pltpu
from jax.sharding import PartitionSpec as P

RAMP = 24
CUTS = 1
NY, NX, NZ, NC = 8, 4, 2, 2
MESH = pl.DeviceIdType.MESH
F32 = jnp.float32
NT = (((1,), (1,)), ((), ()))
NN = (((1,), (0,)), ((), ()))


def far_first(n):
    return sorted(range(1, n), key=lambda d: -min(d, n - d))


def make_kernel(n_freq, r_dev, src, k_dev):
    n_plane = NX * NZ
    rows = n_plane * r_dev
    n_bins = 2 * NY * n_plane
    half = NY // 2
    tail = src - 128

    def kernel(rec, mir, live_hbm, bins_hbm, wts_hbm, lo_hbm, hi_hbm, gain_hbm, out,
               live, bins, wts, lo, hi, gain, raw, sbuf, rraw, rsend, rbuf, meta, mapt, tap, acc, asend, abuf, bsend, bbuf, esend, ebuf,
               l_sem, p_sem, q_sem, word_p, word_f, s_send, s_recv, r_send, r_recv, m_send, m_recv,
               a_send, a_recv, b_send, b_recv, e_send, e_recv):
        blk = lax.axis_index("blk")
        frq = lax.axis_index("freq")
        y = blk // n_plane
        p = blk % n_plane
        x = p // NZ
        z = p % NZ

        core = frq % NC
        deep = (frq // NC) * NZ + z
        nz = (n_freq // NC) * NZ

        offsets = [(dx, dz) for dx in range(NX) for dz in range(NZ) if dx or dz]
        offsets.sort(key=lambda o: min(o[0], NX - o[0]) + o[1])

        def plane_of(dx, dz):
            return ((x + dx) % NX) * NZ + (z + dz) % NZ

        peers = [plane_of(dx, dz) for dx, dz in offsets]
        y_of = [(y + d) % NY for d in range(NY)]
        f_of = [(frq + d) % n_freq for d in range(n_freq)]

        near_y = [(y_of[d] * n_plane + p, frq) for d in (1, NY - 1)]
        near_plane = []
        for d in sorted({1 % NX, NX - 1} - {0}):
            near_plane.append((y * n_plane + ((x + d) % NX) * NZ + z, frq))
        if NZ == 2:
            near_plane.append((y * n_plane + x * NZ + 1 - z, frq))
        near_freq = []
        for d in sorted({1 % nz, nz - 1} - {0}):
            at = (deep + d) % nz
            near_freq.append((y * n_plane + x * NZ + at % NZ, (at // NZ) * NC + core))
        if NC == 2:
            near_freq.append((blk, frq - core + 1 - core))

        barrier = pltpu.get_barrier_semaphore()
        for to in near_y + near_plane + near_freq:
            pl.semaphore_signal(barrier, inc=1, device_id=to, device_id_type=MESH)

        loads = [pltpu.make_async_copy(mir.at[0, c], raw.at[c], l_sem.at[c]) for c in range(2)]
        small = [(live_hbm, live), (bins_hbm, bins), (wts_hbm, wts), (lo_hbm, lo), (hi_hbm, hi), (gain_hbm, gain)]
        small = [pltpu.make_async_copy(a, b, p_sem.at[i]) for i, (a, b) in enumerate(small)]
        small[0].start()
        rows_in = pltpu.make_async_copy(rec.at[0], rraw, q_sem)
        for copy in loads + [rows_in] + small[1:]:
            copy.start()

        small[0].wait()
        on = lax.broadcasted_iota(jnp.int32, (src, k_dev), 1) < live[...]
        for c in range(2):
            loads[c].wait()
            sbuf[y, c] = jnp.where(on, raw[c], jnp.zeros_like(raw[c]))

        pl.semaphore_wait(barrier, len(near_y) + len(near_plane) + len(near_freq))

        n_piece = 2 * CUTS
        piece = src // CUTS

        def ring(way, step, i, landing=False):
            owner = y - step - landing if way == 0 else y + step + landing
            part = i if way == 0 else n_piece - 1 - i
            ref = sbuf.at[(owner + NY) % NY, part // CUTS, pl.ds(part % CUTS * piece, piece), :]
            return pltpu.make_async_remote_copy(
                src_ref=ref, dst_ref=ref,
                send_sem=s_send.at[way, step * n_piece + i], recv_sem=s_recv.at[way, step * n_piece + i],
                device_id=near_y[way], device_id_type=MESH)

        def pieces(step):
            return n_piece // 2 if step == half - 1 else n_piece

        for i in range(n_piece):
            for way in range(2):
                ring(way, 0, i).start()

        def tell(word, near, i):
            for to in near:
                pl.semaphore_signal(word.at[i], inc=1, device_id=to, device_id_type=MESH)

        def heard(word, near, i):
            pl.semaphore_wait(word.at[i], len(near))

        tell(word_p, near_plane, 0)
        tell(word_f, near_freq, 0)

        rows_in.wait()
        for q in range(n_plane):
            for yy in range(NY):
                at = (yy * n_plane + q) * k_dev
                rsend[q, yy] = rraw[:, :, at:at + k_dev]
        rbuf[p] = rsend[p]

        def rows_copy(i, landing=False):
            dx, dz = offsets[i]
            dst = rbuf.at[plane_of(-dx, -dz) if landing else p]
            return pltpu.make_async_remote_copy(
                src_ref=dst if landing else rsend.at[peers[i]], dst_ref=dst,
                send_sem=r_send.at[i], recv_sem=r_recv.at[i],
                device_id=(y * n_plane + peers[i], frq), device_id_type=MESH)

        def hops(i):
            return min(offsets[i][0], NX - offsets[i][0]) + offsets[i][1]

        def send_rows(far):
            for i in range(len(peers)):
                if hops(i) == far:
                    rows_copy(i).start()

        send_rows(1)

        for copy in small[1:]:
            copy.wait()

        def column(line):
            line = jnp.broadcast_to(line.astype(F32), (r_dev, r_dev))
            on = lax.broadcasted_iota(jnp.int32, (r_dev, r_dev), 0) == lax.broadcasted_iota(jnp.int32, (r_dev, r_dev), 1)
            return jnp.sum(jnp.where(on, line, 0.0), axis=1, keepdims=True)

        lane = lax.broadcasted_iota(jnp.int32, (r_dev, 128), 1)
        table = jnp.zeros((r_dev, 128), F32)
        for i, line in enumerate([bins[0:1], bins[1:2], wts[0:1], wts[1:2], lo[...], hi[...]]):
            table = jnp.where(lane == i, column(line), table)
        mine = pl.ds(pl.multiple_of(p * r_dev, r_dev), r_dev)
        meta[mine, :] = table

        def meta_copy(i):
            return pltpu.make_async_remote_copy(
                src_ref=meta.at[mine, :], dst_ref=meta.at[mine, :],
                send_sem=m_send.at[i], recv_sem=m_recv.at[i],
                device_id=(y * n_plane + peers[i], frq), device_id_type=MESH)

        def pass_on(step):
            for i in range(pieces(step)):
                for way in range(2):
                    ring(way, step, i, landing=True).wait_recv()
                    if step + 1 < half and i < pieces(step + 1):
                        ring(way, step + 1, i).start()

        def from_peer(i):
            dx, dz = offsets[i]
            q = plane_of(-dx, -dz)
            rows_q = pl.ds(pl.multiple_of(q * r_dev, r_dev), r_dev)
            pltpu.make_async_remote_copy(
                src_ref=meta.at[rows_q, :], dst_ref=meta.at[rows_q, :],
                send_sem=m_send.at[i], recv_sem=m_recv.at[i],
                device_id=(y * n_plane + peers[i], frq), device_id_type=MESH).wait_recv()

        pass_on(0)
        heard(word_p, near_plane, 0)
        tell(word_p, near_plane, 1)
        send_rows(2)
        if half > 2:
            pass_on(1)
        heard(word_p, near_plane, 1)
        send_rows(3)
        for i in range(len(peers)):
            meta_copy(i).start()
        heard(word_f, near_freq, 0)
        tell(word_f, near_freq, 1)
        for step in range(2, half - 1):
            pass_on(step)
        heard(word_f, near_freq, 1)
        tell(word_f, near_freq, 2)

        for i in range(len(peers)):
            from_peer(i)
        info = meta[...]
        place = lax.broadcasted_iota(jnp.int32, (rows, n_bins), 1)
        per = 2 * NY
        named = (place % per // 2) * (2 * n_plane) + (place // per) * 2 + place % 2
        named = named.astype(F32)
        spread = jnp.where(info[:, 0:1] == named, info[:, 2:3], 0.0) + jnp.where(info[:, 1:2] == named, info[:, 3:4], 0.0)
        mapt[...] = spread.T
        at = lax.broadcasted_iota(jnp.int32, (rows, src), 1).astype(F32)
        rise = jnp.clip((at - info[:, 4:5] + 1.0) / RAMP, 0.0, 1.0)
        fall = jnp.clip((info[:, 5:6] - at) / RAMP, 0.0, 1.0)
        tap[...] = rise * fall

        for i in range(len(peers)):
            rows_copy(i, landing=True).wait_recv()

        def product(d, first=False):
            yy = y_of[d % NY]
            left = rbuf[:, yy].reshape(2 * rows, k_dev)
            for c in range(2):
                part = lax.dot_general(left, sbuf[yy, c], NT, preferred_element_type=F32)
                if first:
                    acc[c] = part
                else:
                    acc[c] += part

        for i, d in enumerate([0] + [s * k for k in range(1, half) for s in (1, -1)]):
            product(d, first=i == 0)
        heard(word_f, near_freq, 2)
        tell(word_f, near_freq, 3)
        pass_on(half - 1)
        product(half)

        def of(c, part):
            return acc[c].reshape(n_plane, 2, r_dev, src)[:, part].reshape(rows, src)

        binned = []
        for c in range(2):
            if c == 0:
                value = of(0, 0) - of(1, 1)
            else:
                value = of(1, 0) + of(0, 1)
            binned.append(lax.dot_general(mapt[...], value * tap[...], NN, precision=lax.Precision.HIGHEST, preferred_element_type=F32))
        asend[:, 0:128] = binned[0][:, 0:128]
        asend[:, 128:256] = binned[1][:, 0:128]
        asend[:, 256:256 + tail] = binned[0][:, 128:src]
        asend[:, 256 + tail:256 + 2 * tail] = binned[1][:, 128:src]

        def a_copy(i):
            to = pl.ds(pl.multiple_of(peers[i] * per, per), per)
            return pltpu.make_async_remote_copy(
                src_ref=asend.at[to, :], dst_ref=abuf.at[i],
                send_sem=a_send.at[i], recv_sem=a_recv.at[i],
                device_id=(y * n_plane + peers[i], frq), device_id_type=MESH)

        for i in reversed(range(len(peers))):
            a_copy(i).start()
        total = asend[pl.ds(pl.multiple_of(p * per, per), per), :]
        for i in range(len(peers)):
            a_copy(i).wait_recv()
            total = total + abuf[i]

        bsend[...] = jnp.zeros_like(bsend)
        for d in range(NY):
            for k in range(3):
                bsend[d, 2 * k:2 * k + 2, :] = total[2 * d:2 * d + 2, 128 * k:128 * k + 128]

        def b_copy(d):
            return pltpu.make_async_remote_copy(
                src_ref=bsend.at[y_of[d]], dst_ref=bbuf.at[d - 1],
                send_sem=b_send.at[d - 1], recv_sem=b_recv.at[d - 1],
                device_id=(y_of[d] * n_plane + p, frq), device_id_type=MESH)

        for d in far_first(NY):
            b_copy(d).start()
        tile = bsend[y]
        for d in range(1, NY):
            b_copy(d).wait_recv()
            tile = tile + bbuf[d - 1]
        scaled = tile * gain[...]
        square = scaled * scaled
        esend[...] = square

        def e_copy(d):
            return pltpu.make_async_remote_copy(
                src_ref=esend, dst_ref=ebuf.at[d - 1],
                send_sem=e_send.at[d - 1], recv_sem=e_recv.at[d - 1],
                device_id=(blk, f_of[d]), device_id_type=MESH)

        heard(word_f, near_freq, 3)
        for d in far_first(n_freq):
            e_copy(d).start()
        for step in range(half):
            for i in range(pieces(step)):
                for way in range(2):
                    ring(way, step, i).wait_send()
        for i in range(len(peers)):
            rows_copy(i).wait_send()
            meta_copy(i).wait_send()
            a_copy(i).wait_send()
        for d in range(1, NY):
            b_copy(d).wait_send()
        for d in range(1, n_freq):
            e_copy(d).wait_recv()
            square = square + ebuf[d - 1]
        for d in range(1, n_freq):
            e_copy(d).wait_send()
        energy = jnp.sum(square[0:2] + square[2:4] + square[4:6], axis=1, keepdims=True)
        norm = jnp.sqrt(energy / (n_freq * 2 * src) + 1e-06)
        for c in range(2):
            out[0, c, :, 0:128] = scaled[2 * c:2 * c + 2] / norm
            out[0, c, :, 128:src] = scaled[4:6, c * tail:(c + 1) * tail] / norm

    return kernel


def solution(mesh):
    n_freq = mesh.shape["freq"]

    def local(recorded, mirror, live_counts, bins, bin_weight, taper_lo, taper_hi, gain):
        r_dev = recorded.shape[2]
        src, k_dev = mirror.shape[2], mirror.shape[3]
        n_plane = NX * NZ
        rows, per, n_peer, half = n_plane * r_dev, 2 * NY, n_plane - 1, NY // 2
        hbm, vmem = (pl.BlockSpec(memory_space=m) for m in (pltpu.HBM, pltpu.VMEM))
        dma = pltpu.SemaphoreType.DMA
        bf16 = jnp.bfloat16
        return pl.pallas_call(
            make_kernel(n_freq, r_dev, src, k_dev),
            out_shape=jax.ShapeDtypeStruct((1, 2, 2, src), F32),
            in_specs=[hbm] * 8,
            out_specs=vmem,
            scratch_shapes=[
                pltpu.VMEM((1, 1), jnp.int32),
                pltpu.VMEM((2, r_dev), jnp.int32),
                pltpu.VMEM((2, r_dev), F32),
                pltpu.VMEM((1, r_dev), jnp.int32),
                pltpu.VMEM((1, r_dev), jnp.int32),
                pltpu.VMEM((1, 1), F32),
                pltpu.VMEM((2, src, k_dev), bf16),
                pltpu.VMEM((NY, 2, src, k_dev), bf16),
                pltpu.VMEM((2, r_dev, NY * n_plane * k_dev), bf16),
                pltpu.VMEM((n_plane, NY, 2, r_dev, k_dev), bf16),
                pltpu.VMEM((n_plane, NY, 2, r_dev, k_dev), bf16),
                pltpu.VMEM((rows, 128), F32),
                pltpu.VMEM((2 * NY * n_plane, rows), F32),
                pltpu.VMEM((rows, src), F32),
                pltpu.VMEM((2, 2 * rows, src), F32),
                pltpu.VMEM((per * n_plane, 2 * src), F32),
                pltpu.VMEM((n_peer, per, 2 * src), F32),
                pltpu.VMEM((NY, 8, 128), F32),
                pltpu.VMEM((NY - 1, 8, 128), F32),
                pltpu.VMEM((8, 128), F32),
                pltpu.VMEM((n_freq - 1, 8, 128), F32),
                dma((2,)), dma((6,)), dma, pltpu.SemaphoreType.REGULAR((2,)), pltpu.SemaphoreType.REGULAR((4,)),
                dma((2, 2 * CUTS * half)), dma((2, 2 * CUTS * half)),
                dma((n_peer,)), dma((n_peer,)),
                dma((n_peer,)), dma((n_peer,)),
                dma((n_peer,)), dma((n_peer,)),
                dma((NY - 1,)), dma((NY - 1,)),
                dma((n_freq - 1,)), dma((n_freq - 1,)),
            ],
            compiler_params=pltpu.CompilerParams(
                collective_id=0, has_side_effects=True, vmem_limit_bytes=55150 * 1024
            ),
        )(recorded, mirror, live_counts, bins[0].T, bin_weight[0].T, taper_lo, taper_hi, gain.reshape(1, 1))

    in_specs = (
        P("freq", None, "blk", None),
        P("freq", None, None, "blk"),
        P("freq", "blk"),
        P("freq", "blk", None),
        P("freq", "blk", None),
        P("freq", "blk"),
        P("freq", "blk"),
        P("freq"),
    )
    out_specs = P("freq", None, "blk", None)
    return jax.shard_map(local, mesh=mesh, in_specs=in_specs, out_specs=out_specs, check_vma=False)
```

```python
import jax
import jax.numpy as jnp
from jax import lax
from jax.experimental import pallas as pl
from jax.experimental.pallas import tpu as pltpu
from jax.sharding import PartitionSpec as P

RAMP = 24
CUTS = 1
NY, NX, NZ, NC = 8, 4, 2, 2
MESH = pl.DeviceIdType.MESH
F32 = jnp.float32
NT = (((1,), (1,)), ((), ()))
NN = (((1,), (0,)), ((), ()))


def far_first(n):
    return sorted(range(1, n), key=lambda d: -min(d, n - d))


def make_kernel(n_freq, r_dev, src, k_dev):
    n_plane = NX * NZ
    rows = n_plane * r_dev
    n_bins = 2 * NY * n_plane
    half = NY // 2
    tail = src - 128

    def kernel(rec, mir, live_hbm, bins_hbm, wts_hbm, lo_hbm, hi_hbm, gain_hbm, out,
               live, bins, wts, lo, hi, gain, raw, sbuf, rraw, rsend, rbuf, meta, mapt, tap, acc, asend, abuf, bsend, bbuf, esend, ebuf,
               l_sem, p_sem, q_sem, word_p, word_f, s_send, s_recv, r_send, r_recv, m_send, m_recv,
               a_send, a_recv, b_send, b_recv, e_send, e_recv):
        blk = lax.axis_index("blk")
        frq = lax.axis_index("freq")
        y = blk // n_plane
        p = blk % n_plane
        x = p // NZ
        z = p % NZ

        core = frq % NC
        deep = (frq // NC) * NZ + z
        nz = (n_freq // NC) * NZ

        offsets = [(dx, dz) for dx in range(NX) for dz in range(NZ) if dx or dz]
        offsets.sort(key=lambda o: min(o[0], NX - o[0]) + o[1])

        def plane_of(dx, dz):
            return ((x + dx) % NX) * NZ + (z + dz) % NZ

        peers = [plane_of(dx, dz) for dx, dz in offsets]
        y_of = [(y + d) % NY for d in range(NY)]
        f_of = [(frq + d) % n_freq for d in range(n_freq)]

        near_y = [(y_of[d] * n_plane + p, frq) for d in (1, NY - 1)]
        near_plane = []
        for d in sorted({1 % NX, NX - 1} - {0}):
            near_plane.append((y * n_plane + ((x + d) % NX) * NZ + z, frq))
        if NZ == 2:
            near_plane.append((y * n_plane + x * NZ + 1 - z, frq))
        near_freq = []
        for d in sorted({1 % nz, nz - 1} - {0}):
            at = (deep + d) % nz
            near_freq.append((y * n_plane + x * NZ + at % NZ, (at // NZ) * NC + core))
        if NC == 2:
            near_freq.append((blk, frq - core + 1 - core))

        barrier = pltpu.get_barrier_semaphore()
        for to in near_y + near_plane + near_freq:
            pl.semaphore_signal(barrier, inc=1, device_id=to, device_id_type=MESH)

        loads = [pltpu.make_async_copy(mir.at[0, c], raw.at[c], l_sem.at[c]) for c in range(2)]
        small = [(live_hbm, live), (bins_hbm, bins), (wts_hbm, wts), (lo_hbm, lo), (hi_hbm, hi), (gain_hbm, gain)]
        small = [pltpu.make_async_copy(a, b, p_sem.at[i]) for i, (a, b) in enumerate(small)]
        small[0].start()
        rows_in = pltpu.make_async_copy(rec.at[0], rraw, q_sem)
        for copy in loads + [rows_in] + small[1:]:
            copy.start()

        small[0].wait()
        on = lax.broadcasted_iota(jnp.int32, (src, k_dev), 1) < live[...]
        for c in range(2):
            loads[c].wait()
            sbuf[y, c] = jnp.where(on, raw[c], jnp.zeros_like(raw[c]))

        pl.semaphore_wait(barrier, len(near_y) + len(near_plane) + len(near_freq))

        n_piece = 2 * CUTS
        piece = src // CUTS

        def ring(way, step, i, landing=False):
            owner = y - step - landing if way == 0 else y + step + landing
            part = i if way == 0 else n_piece - 1 - i
            ref = sbuf.at[(owner + NY) % NY, part // CUTS, pl.ds(part % CUTS * piece, piece), :]
            return pltpu.make_async_remote_copy(
                src_ref=ref, dst_ref=ref,
                send_sem=s_send.at[way, step * n_piece + i], recv_sem=s_recv.at[way, step * n_piece + i],
                device_id=near_y[way], device_id_type=MESH)

        def pieces(step):
            return n_piece // 2 if step == half - 1 else n_piece

        for i in range(n_piece):
            for way in range(2):
                ring(way, 0, i).start()

        def tell(word, near, i):
            for to in near:
                pl.semaphore_signal(word.at[i], inc=1, device_id=to, device_id_type=MESH)

        def heard(word, near, i):
            pl.semaphore_wait(word.at[i], len(near))

        bsend[...] = jnp.zeros_like(bsend)
        tell(word_p, near_plane, 0)
        tell(word_f, near_freq, 0)

        rows_in.wait()
        for q in range(n_plane):
            for yy in range(NY):
                at = (yy * n_plane + q) * k_dev
                rsend[q, yy] = rraw[:, :, at:at + k_dev]
        rbuf[p] = rsend[p]

        def rows_copy(i, landing=False):
            dx, dz = offsets[i]
            dst = rbuf.at[plane_of(-dx, -dz) if landing else p]
            return pltpu.make_async_remote_copy(
                src_ref=dst if landing else rsend.at[peers[i]], dst_ref=dst,
                send_sem=r_send.at[i], recv_sem=r_recv.at[i],
                device_id=(y * n_plane + peers[i], frq), device_id_type=MESH)

        def meta_copy(i):
            return pltpu.make_async_remote_copy(
                src_ref=meta.at[mine, :], dst_ref=meta.at[mine, :],
                send_sem=m_send.at[i], recv_sem=m_recv.at[i],
                device_id=(y * n_plane + peers[i], frq), device_id_type=MESH)

        def hops(i):
            return min(offsets[i][0], NX - offsets[i][0]) + offsets[i][1]

        def send_rows(far):
            for i in range(len(peers)):
                if hops(i) == far:
                    meta_copy(i).start()
                    rows_copy(i).start()


        for copy in small[1:]:
            copy.wait()

        def column(line):
            line = jnp.broadcast_to(line.astype(F32), (r_dev, r_dev))
            on = lax.broadcasted_iota(jnp.int32, (r_dev, r_dev), 0) == lax.broadcasted_iota(jnp.int32, (r_dev, r_dev), 1)
            return jnp.sum(jnp.where(on, line, 0.0), axis=1, keepdims=True)

        lane = lax.broadcasted_iota(jnp.int32, (r_dev, 128), 1)
        table = jnp.zeros((r_dev, 128), F32)
        for i, line in enumerate([bins[0:1], bins[1:2], wts[0:1], wts[1:2], lo[...], hi[...]]):
            table = jnp.where(lane == i, column(line), table)
        mine = pl.ds(pl.multiple_of(p * r_dev, r_dev), r_dev)
        meta[mine, :] = table

        send_rows(1)

        def pass_on(step):
            for i in range(pieces(step)):
                for way in range(2):
                    ring(way, step, i, landing=True).wait_recv()
                    if step + 1 < half and i < pieces(step + 1):
                        ring(way, step + 1, i).start()

        def from_peer(i):
            dx, dz = offsets[i]
            q = plane_of(-dx, -dz)
            rows_q = pl.ds(pl.multiple_of(q * r_dev, r_dev), r_dev)
            pltpu.make_async_remote_copy(
                src_ref=meta.at[rows_q, :], dst_ref=meta.at[rows_q, :],
                send_sem=m_send.at[i], recv_sem=m_recv.at[i],
                device_id=(y * n_plane + peers[i], frq), device_id_type=MESH).wait_recv()

        heard(word_p, near_plane, 0)
        tell(word_p, near_plane, 1)
        send_rows(2)
        pass_on(0)
        if half > 2:
            pass_on(1)
        heard(word_p, near_plane, 1)
        send_rows(3)
        heard(word_f, near_freq, 0)
        tell(word_f, near_freq, 1)
        for step in range(2, half - 1):
            pass_on(step)
        heard(word_f, near_freq, 1)
        tell(word_f, near_freq, 2)

        for i in range(len(peers)):
            from_peer(i)
        info = meta[...]
        place = lax.broadcasted_iota(jnp.int32, (rows, n_bins), 1)
        per = 2 * NY
        named = (place % per // 2) * (2 * n_plane) + (place // per) * 2 + place % 2
        named = named.astype(F32)
        spread = jnp.where(info[:, 0:1] == named, info[:, 2:3], 0.0) + jnp.where(info[:, 1:2] == named, info[:, 3:4], 0.0)
        mapt[...] = spread.T
        at = lax.broadcasted_iota(jnp.int32, (rows, src), 1).astype(F32)
        rise = jnp.clip((at - info[:, 4:5] + 1.0) / RAMP, 0.0, 1.0)
        fall = jnp.clip((info[:, 5:6] - at) / RAMP, 0.0, 1.0)
        tap[...] = rise * fall


        for i in range(len(peers)):
            rows_copy(i, landing=True).wait_recv()

        def product(blocks):
            at = [y_of[d % NY] for d in blocks]
            left = jnp.concatenate([rbuf[:, yy].reshape(2 * rows, k_dev) for yy in at], axis=1)
            return [lax.dot_general(left, jnp.concatenate([sbuf[yy, c] for yy in at], axis=1), NT, preferred_element_type=F32)
                    for c in range(2)]

        for c, part in enumerate(product([d for d in range(NY) if d != half])):
            acc[c] = part
        heard(word_f, near_freq, 2)
        tell(word_f, near_freq, 3)
        pass_on(half - 1)
        for c, part in enumerate(product([half])):
            acc[c] += part

        def of(c, part):
            return acc[c].reshape(n_plane, 2, r_dev, src)[:, part].reshape(rows, src)

        binned = []
        for c in range(2):
            if c == 0:
                value = of(0, 0) - of(1, 1)
            else:
                value = of(1, 0) + of(0, 1)
            binned.append(lax.dot_general(mapt[...], value * tap[...], NN, precision=lax.Precision.HIGHEST, preferred_element_type=F32))
        asend[:, 0:128] = binned[0][:, 0:128]
        asend[:, 128:256] = binned[1][:, 0:128]
        asend[:, 256:256 + tail] = binned[0][:, 128:src]
        asend[:, 256 + tail:256 + 2 * tail] = binned[1][:, 128:src]

        def a_copy(i):
            to = pl.ds(pl.multiple_of(peers[i] * per, per), per)
            return pltpu.make_async_remote_copy(
                src_ref=asend.at[to, :], dst_ref=abuf.at[i],
                send_sem=a_send.at[i], recv_sem=a_recv.at[i],
                device_id=(y * n_plane + peers[i], frq), device_id_type=MESH)

        for i in reversed(range(len(peers))):
            a_copy(i).start()
        total = asend[pl.ds(pl.multiple_of(p * per, per), per), :]
        for i in range(len(peers)):
            a_copy(i).wait_recv()
            total = total + abuf[i]

        for d in range(NY):
            for k in range(3):
                bsend[d, 2 * k:2 * k + 2, :] = total[2 * d:2 * d + 2, 128 * k:128 * k + 128]

        def b_copy(d):
            return pltpu.make_async_remote_copy(
                src_ref=bsend.at[y_of[d]], dst_ref=bbuf.at[d - 1],
                send_sem=b_send.at[d - 1], recv_sem=b_recv.at[d - 1],
                device_id=(y_of[d] * n_plane + p, frq), device_id_type=MESH)

        for d in far_first(NY):
            b_copy(d).start()
        tile = bsend[y]
        for d in range(1, NY):
            b_copy(d).wait_recv()
            tile = tile + bbuf[d - 1]
        scaled = tile * gain[...]
        square = scaled * scaled
        esend[...] = square

        def e_copy(d):
            return pltpu.make_async_remote_copy(
                src_ref=esend, dst_ref=ebuf.at[d - 1],
                send_sem=e_send.at[d - 1], recv_sem=e_recv.at[d - 1],
                device_id=(blk, f_of[d]), device_id_type=MESH)

        heard(word_f, near_freq, 3)
        for d in far_first(n_freq):
            e_copy(d).start()
        for step in range(half):
            for i in range(pieces(step)):
                for way in range(2):
                    ring(way, step, i).wait_send()
        for i in range(len(peers)):
            rows_copy(i).wait_send()
            meta_copy(i).wait_send()
            a_copy(i).wait_send()
        for d in range(1, NY):
            b_copy(d).wait_send()
        for d in range(1, n_freq):
            e_copy(d).wait_recv()
            square = square + ebuf[d - 1]
        for d in range(1, n_freq):
            e_copy(d).wait_send()
        energy = jnp.sum(square[0:2] + square[2:4] + square[4:6], axis=1, keepdims=True)
        norm = jnp.sqrt(energy / (n_freq * 2 * src) + 1e-06)
        for c in range(2):
            out[0, c, :, 0:128] = scaled[2 * c:2 * c + 2] / norm
            out[0, c, :, 128:src] = scaled[4:6, c * tail:(c + 1) * tail] / norm

    return kernel


def solution(mesh):
    n_freq = mesh.shape["freq"]

    def local(recorded, mirror, live_counts, bins, bin_weight, taper_lo, taper_hi, gain):
        r_dev = recorded.shape[2]
        src, k_dev = mirror.shape[2], mirror.shape[3]
        n_plane = NX * NZ
        rows, per, n_peer, half = n_plane * r_dev, 2 * NY, n_plane - 1, NY // 2
        hbm, vmem = (pl.BlockSpec(memory_space=m) for m in (pltpu.HBM, pltpu.VMEM))
        dma = pltpu.SemaphoreType.DMA
        bf16 = jnp.bfloat16
        return pl.pallas_call(
            make_kernel(n_freq, r_dev, src, k_dev),
            out_shape=jax.ShapeDtypeStruct((1, 2, 2, src), F32),
            in_specs=[hbm] * 8,
            out_specs=vmem,
            scratch_shapes=[
                pltpu.VMEM((1, 1), jnp.int32),
                pltpu.VMEM((2, r_dev), jnp.int32),
                pltpu.VMEM((2, r_dev), F32),
                pltpu.VMEM((1, r_dev), jnp.int32),
                pltpu.VMEM((1, r_dev), jnp.int32),
                pltpu.VMEM((1, 1), F32),
                pltpu.VMEM((2, src, k_dev), bf16),
                pltpu.VMEM((NY, 2, src, k_dev), bf16),
                pltpu.VMEM((2, r_dev, NY * n_plane * k_dev), bf16),
                pltpu.VMEM((n_plane, NY, 2, r_dev, k_dev), bf16),
                pltpu.VMEM((n_plane, NY, 2, r_dev, k_dev), bf16),
                pltpu.VMEM((rows, 128), F32),
                pltpu.VMEM((2 * NY * n_plane, rows), F32),
                pltpu.VMEM((rows, src), F32),
                pltpu.VMEM((2, 2 * rows, src), F32),
                pltpu.VMEM((per * n_plane, 2 * src), F32),
                pltpu.VMEM((n_peer, per, 2 * src), F32),
                pltpu.VMEM((NY, 8, 128), F32),
                pltpu.VMEM((NY - 1, 8, 128), F32),
                pltpu.VMEM((8, 128), F32),
                pltpu.VMEM((n_freq - 1, 8, 128), F32),
                dma((2,)), dma((6,)), dma, pltpu.SemaphoreType.REGULAR((2,)), pltpu.SemaphoreType.REGULAR((4,)),
                dma((2, 2 * CUTS * half)), dma((2, 2 * CUTS * half)),
                dma((n_peer,)), dma((n_peer,)),
                dma((n_peer,)), dma((n_peer,)),
                dma((n_peer,)), dma((n_peer,)),
                dma((NY - 1,)), dma((NY - 1,)),
                dma((n_freq - 1,)), dma((n_freq - 1,)),
            ],
            compiler_params=pltpu.CompilerParams(
                collective_id=0, has_side_effects=True, vmem_limit_bytes=55150 * 1024
            ),
        )(recorded, mirror, live_counts, bins[0].T, bin_weight[0].T, taper_lo, taper_hi, gain.reshape(1, 1))

    in_specs = (
        P("freq", None, "blk", None),
        P("freq", None, None, "blk"),
        P("freq", "blk"),
        P("freq", "blk", None),
        P("freq", "blk", None),
        P("freq", "blk"),
        P("freq", "blk"),
        P("freq"),
    )
    out_specs = P("freq", None, "blk", None)
    return jax.shard_map(local, mesh=mesh, in_specs=in_specs, out_specs=out_specs, check_vma=False)
```

```python
import jax
import jax.numpy as jnp
from jax import lax
from jax.experimental import pallas as pl
from jax.experimental.pallas import tpu as pltpu
from jax.sharding import PartitionSpec as P

RAMP = 24
CUTS = 1
NY, NX, NZ, NC = 8, 4, 2, 2
MESH = pl.DeviceIdType.MESH
F32 = jnp.float32
NT = (((1,), (1,)), ((), ()))
NN = (((1,), (0,)), ((), ()))


def far_first(n):
    return sorted(range(1, n), key=lambda d: -min(d, n - d))


def make_kernel(n_freq, r_dev, src, k_dev):
    n_plane = NX * NZ
    rows = n_plane * r_dev
    n_bins = 2 * NY * n_plane
    half = NY // 2
    tail = src - 128

    def kernel(rec, mir, live_hbm, bins_hbm, wts_hbm, lo_hbm, hi_hbm, gain_hbm, out,
               live, bins, wts, lo, hi, gain, raw, sbuf, rraw, rsend, rbuf, meta, mapt, tap, acc, asend, abuf, bsend, bbuf, esend, ebuf,
               l_sem, p_sem, q_sem, word_p, word_f, s_send, s_recv, r_send, r_recv, m_send, m_recv,
               a_send, a_recv, b_send, b_recv, e_send, e_recv):
        blk = lax.axis_index("blk")
        frq = lax.axis_index("freq")
        y = blk // n_plane
        p = blk % n_plane
        x = p // NZ
        z = p % NZ

        core = frq % NC
        deep = (frq // NC) * NZ + z
        nz = (n_freq // NC) * NZ

        offsets = [(dx, dz) for dx in range(NX) for dz in range(NZ) if dx or dz]
        offsets.sort(key=lambda o: min(o[0], NX - o[0]) + o[1])

        def plane_of(dx, dz):
            return ((x + dx) % NX) * NZ + (z + dz) % NZ

        peers = [plane_of(dx, dz) for dx, dz in offsets]
        y_of = [(y + d) % NY for d in range(NY)]
        f_of = [(frq + d) % n_freq for d in range(n_freq)]

        near_y = [(y_of[d] * n_plane + p, frq) for d in (1, NY - 1)]
        near_plane = []
        for d in sorted({1 % NX, NX - 1} - {0}):
            near_plane.append((y * n_plane + ((x + d) % NX) * NZ + z, frq))
        if NZ == 2:
            near_plane.append((y * n_plane + x * NZ + 1 - z, frq))
        near_freq = []
        for d in sorted({1 % nz, nz - 1} - {0}):
            at = (deep + d) % nz
            near_freq.append((y * n_plane + x * NZ + at % NZ, (at // NZ) * NC + core))
        if NC == 2:
            near_freq.append((blk, frq - core + 1 - core))

        barrier = pltpu.get_barrier_semaphore()
        for to in near_y + near_plane + near_freq:
            pl.semaphore_signal(barrier, inc=1, device_id=to, device_id_type=MESH)

        loads = [pltpu.make_async_copy(mir.at[0, c], raw.at[c], l_sem.at[c]) for c in range(2)]
        small = [(live_hbm, live), (bins_hbm, bins), (wts_hbm, wts), (lo_hbm, lo), (hi_hbm, hi), (gain_hbm, gain)]
        small = [pltpu.make_async_copy(a, b, p_sem.at[i]) for i, (a, b) in enumerate(small)]
        small[0].start()
        rows_in = pltpu.make_async_copy(rec.at[0], rraw, q_sem)
        for copy in loads + [rows_in] + small[1:]:
            copy.start()

        small[0].wait()
        on = lax.broadcasted_iota(jnp.int32, (src, k_dev), 1) < live[...]
        for c in range(2):
            loads[c].wait()
            sbuf[y, c] = jnp.where(on, raw[c], jnp.zeros_like(raw[c]))

        pl.semaphore_wait(barrier, len(near_y) + len(near_plane) + len(near_freq))

        n_piece = 2 * CUTS
        piece = src // CUTS

        def ring(way, step, i, landing=False):
            owner = y - step - landing if way == 0 else y + step + landing
            part = i if way == 0 else n_piece - 1 - i
            ref = sbuf.at[(owner + NY) % NY, part // CUTS, pl.ds(part % CUTS * piece, piece), :]
            return pltpu.make_async_remote_copy(
                src_ref=ref, dst_ref=ref,
                send_sem=s_send.at[way, step * n_piece + i], recv_sem=s_recv.at[way, step * n_piece + i],
                device_id=near_y[way], device_id_type=MESH)

        def pieces(step):
            return n_piece // 2 if step == half - 1 else n_piece

        for i in range(n_piece):
            for way in range(2):
                ring(way, 0, i).start()

        def tell(word, near, i):
            for to in near:
                pl.semaphore_signal(word.at[i], inc=1, device_id=to, device_id_type=MESH)

        def heard(word, near, i):
            pl.semaphore_wait(word.at[i], len(near))

        bsend[...] = jnp.zeros_like(bsend)
        tell(word_p, near_plane, 0)
        tell(word_f, near_freq, 0)

        rows_in.wait()
        for q in range(n_plane):
            for yy in range(NY):
                at = (yy * n_plane + q) * k_dev
                rsend[q, yy] = rraw[:, :, at:at + k_dev]
        rbuf[p] = rsend[p]

        def rows_copy(i, landing=False):
            dx, dz = offsets[i]
            dst = rbuf.at[plane_of(-dx, -dz) if landing else p]
            return pltpu.make_async_remote_copy(
                src_ref=dst if landing else rsend.at[peers[i]], dst_ref=dst,
                send_sem=r_send.at[i], recv_sem=r_recv.at[i],
                device_id=(y * n_plane + peers[i], frq), device_id_type=MESH)

        def meta_copy(i):
            return pltpu.make_async_remote_copy(
                src_ref=meta.at[mine, :], dst_ref=meta.at[mine, :],
                send_sem=m_send.at[i], recv_sem=m_recv.at[i],
                device_id=(y * n_plane + peers[i], frq), device_id_type=MESH)

        def hops(i):
            return min(offsets[i][0], NX - offsets[i][0]) + offsets[i][1]

        def send_rows(far):
            for i in range(len(peers)):
                if hops(i) == far:
                    meta_copy(i).start()
                    rows_copy(i).start()


        for copy in small[1:]:
            copy.wait()

        def column(line):
            line = jnp.broadcast_to(line.astype(F32), (r_dev, r_dev))
            on = lax.broadcasted_iota(jnp.int32, (r_dev, r_dev), 0) == lax.broadcasted_iota(jnp.int32, (r_dev, r_dev), 1)
            return jnp.sum(jnp.where(on, line, 0.0), axis=1, keepdims=True)

        lane = lax.broadcasted_iota(jnp.int32, (r_dev, 128), 1)
        table = jnp.zeros((r_dev, 128), F32)
        for i, line in enumerate([bins[0:1], bins[1:2], wts[0:1], wts[1:2], lo[...], hi[...]]):
            table = jnp.where(lane == i, column(line), table)
        mine = pl.ds(pl.multiple_of(p * r_dev, r_dev), r_dev)
        meta[mine, :] = table

        send_rows(1)

        def pass_on(step):
            for i in range(pieces(step)):
                for way in range(2):
                    ring(way, step, i, landing=True).wait_recv()
                    if step + 1 < half and i < pieces(step + 1):
                        ring(way, step + 1, i).start()

        def from_peer(i):
            dx, dz = offsets[i]
            q = plane_of(-dx, -dz)
            rows_q = pl.ds(pl.multiple_of(q * r_dev, r_dev), r_dev)
            pltpu.make_async_remote_copy(
                src_ref=meta.at[rows_q, :], dst_ref=meta.at[rows_q, :],
                send_sem=m_send.at[i], recv_sem=m_recv.at[i],
                device_id=(y * n_plane + peers[i], frq), device_id_type=MESH).wait_recv()

        heard(word_p, near_plane, 0)
        tell(word_p, near_plane, 1)
        send_rows(2)
        pass_on(0)
        if half > 2:
            pass_on(1)
        heard(word_p, near_plane, 1)
        send_rows(3)
        heard(word_f, near_freq, 0)
        tell(word_f, near_freq, 1)
        for step in range(2, half - 1):
            pass_on(step)
        heard(word_f, near_freq, 1)
        tell(word_f, near_freq, 2)

        for i in range(len(peers)):
            from_peer(i)
        info = meta[...]
        place = lax.broadcasted_iota(jnp.int32, (rows, n_bins), 1)
        per = 2 * NY
        named = (place % per // 2) * (2 * n_plane) + (place // per) * 2 + place % 2
        named = named.astype(F32)
        spread = jnp.where(info[:, 0:1] == named, info[:, 2:3], 0.0) + jnp.where(info[:, 1:2] == named, info[:, 3:4], 0.0)
        mapt[...] = spread.T
        at = lax.broadcasted_iota(jnp.int32, (rows, src), 1).astype(F32)
        rise = jnp.clip((at - info[:, 4:5] + 1.0) / RAMP, 0.0, 1.0)
        fall = jnp.clip((info[:, 5:6] - at) / RAMP, 0.0, 1.0)
        tap[...] = rise * fall


        for i in range(len(peers)):
            rows_copy(i, landing=True).wait_recv()

        def product(blocks):
            at = [y_of[d % NY] for d in blocks]
            left = jnp.concatenate([rbuf[:, yy].reshape(2 * rows, k_dev) for yy in at], axis=1)
            return [lax.dot_general(left, jnp.concatenate([sbuf[yy, c] for yy in at], axis=1), NT, preferred_element_type=F32)
                    for c in range(2)]

        for c, part in enumerate(product([d for d in range(NY) if d != half])):
            acc[c] = part
        pass_on(half - 1)
        for c, part in enumerate(product([half])):
            acc[c] += part

        def of(c, part):
            return acc[c].reshape(n_plane, 2, r_dev, src)[:, part].reshape(rows, src)

        binned = []
        for c in range(2):
            if c == 0:
                value = of(0, 0) - of(1, 1)
            else:
                value = of(1, 0) + of(0, 1)
            value = value * tap[...]
            top = value.astype(jnp.bfloat16)
            low = (value - top.astype(F32)).astype(jnp.bfloat16)
            weight_top = mapt[...].astype(jnp.bfloat16)
            weight_low = (mapt[...] - weight_top.astype(F32)).astype(jnp.bfloat16)
            binned.append(sum(lax.dot_general(m, v, NN, preferred_element_type=F32)
                              for m, v in ((weight_top, low), (weight_low, top), (weight_top, top))))
        asend[:, 0:128] = binned[0][:, 0:128]
        asend[:, 128:256] = binned[1][:, 0:128]
        asend[:, 256:256 + tail] = binned[0][:, 128:src]
        asend[:, 256 + tail:256 + 2 * tail] = binned[1][:, 128:src]

        def a_copy(i):
            to = pl.ds(pl.multiple_of(peers[i] * per, per), per)
            return pltpu.make_async_remote_copy(
                src_ref=asend.at[to, :], dst_ref=abuf.at[i],
                send_sem=a_send.at[i], recv_sem=a_recv.at[i],
                device_id=(y * n_plane + peers[i], frq), device_id_type=MESH)

        for i in reversed(range(len(peers))):
            a_copy(i).start()
        heard(word_f, near_freq, 2)
        tell(word_f, near_freq, 3)
        total = asend[pl.ds(pl.multiple_of(p * per, per), per), :]
        for i in range(len(peers)):
            a_copy(i).wait_recv()
            total = total + abuf[i]

        for d in range(NY):
            for k in range(3):
                bsend[d, 2 * k:2 * k + 2, :] = total[2 * d:2 * d + 2, 128 * k:128 * k + 128]

        def b_copy(d):
            return pltpu.make_async_remote_copy(
                src_ref=bsend.at[y_of[d]], dst_ref=bbuf.at[d - 1],
                send_sem=b_send.at[d - 1], recv_sem=b_recv.at[d - 1],
                device_id=(y_of[d] * n_plane + p, frq), device_id_type=MESH)

        for d in far_first(NY):
            b_copy(d).start()
        tile = bsend[y]
        for d in range(1, NY):
            b_copy(d).wait_recv()
            tile = tile + bbuf[d - 1]
        scaled = tile * gain[...]
        square = scaled * scaled
        esend[...] = square

        def e_copy(d):
            return pltpu.make_async_remote_copy(
                src_ref=esend, dst_ref=ebuf.at[d - 1],
                send_sem=e_send.at[d - 1], recv_sem=e_recv.at[d - 1],
                device_id=(blk, f_of[d]), device_id_type=MESH)

        heard(word_f, near_freq, 3)
        for d in far_first(n_freq):
            e_copy(d).start()
        for step in range(half):
            for i in range(pieces(step)):
                for way in range(2):
                    ring(way, step, i).wait_send()
        for i in range(len(peers)):
            rows_copy(i).wait_send()
            meta_copy(i).wait_send()
            a_copy(i).wait_send()
        for d in range(1, NY):
            b_copy(d).wait_send()
        for d in range(1, n_freq):
            e_copy(d).wait_recv()
            square = square + ebuf[d - 1]
        for d in range(1, n_freq):
            e_copy(d).wait_send()
        energy = jnp.sum(square[0:2] + square[2:4] + square[4:6], axis=1, keepdims=True)
        norm = jnp.sqrt(energy / (n_freq * 2 * src) + 1e-06)
        for c in range(2):
            out[0, c, :, 0:128] = scaled[2 * c:2 * c + 2] / norm
            out[0, c, :, 128:src] = scaled[4:6, c * tail:(c + 1) * tail] / norm

    return kernel


def solution(mesh):
    n_freq = mesh.shape["freq"]

    def local(recorded, mirror, live_counts, bins, bin_weight, taper_lo, taper_hi, gain):
        r_dev = recorded.shape[2]
        src, k_dev = mirror.shape[2], mirror.shape[3]
        n_plane = NX * NZ
        rows, per, n_peer, half = n_plane * r_dev, 2 * NY, n_plane - 1, NY // 2
        hbm, vmem = (pl.BlockSpec(memory_space=m) for m in (pltpu.HBM, pltpu.VMEM))
        dma = pltpu.SemaphoreType.DMA
        bf16 = jnp.bfloat16
        return pl.pallas_call(
            make_kernel(n_freq, r_dev, src, k_dev),
            out_shape=jax.ShapeDtypeStruct((1, 2, 2, src), F32),
            in_specs=[hbm] * 8,
            out_specs=vmem,
            scratch_shapes=[
                pltpu.VMEM((1, 1), jnp.int32),
                pltpu.VMEM((2, r_dev), jnp.int32),
                pltpu.VMEM((2, r_dev), F32),
                pltpu.VMEM((1, r_dev), jnp.int32),
                pltpu.VMEM((1, r_dev), jnp.int32),
                pltpu.VMEM((1, 1), F32),
                pltpu.VMEM((2, src, k_dev), bf16),
                pltpu.VMEM((NY, 2, src, k_dev), bf16),
                pltpu.VMEM((2, r_dev, NY * n_plane * k_dev), bf16),
                pltpu.VMEM((n_plane, NY, 2, r_dev, k_dev), bf16),
                pltpu.VMEM((n_plane, NY, 2, r_dev, k_dev), bf16),
                pltpu.VMEM((rows, 128), F32),
                pltpu.VMEM((2 * NY * n_plane, rows), F32),
                pltpu.VMEM((rows, src), F32),
                pltpu.VMEM((2, 2 * rows, src), F32),
                pltpu.VMEM((per * n_plane, 2 * src), F32),
                pltpu.VMEM((n_peer, per, 2 * src), F32),
                pltpu.VMEM((NY, 8, 128), F32),
                pltpu.VMEM((NY - 1, 8, 128), F32),
                pltpu.VMEM((8, 128), F32),
                pltpu.VMEM((n_freq - 1, 8, 128), F32),
                dma((2,)), dma((6,)), dma, pltpu.SemaphoreType.REGULAR((2,)), pltpu.SemaphoreType.REGULAR((4,)),
                dma((2, 2 * CUTS * half)), dma((2, 2 * CUTS * half)),
                dma((n_peer,)), dma((n_peer,)),
                dma((n_peer,)), dma((n_peer,)),
                dma((n_peer,)), dma((n_peer,)),
                dma((NY - 1,)), dma((NY - 1,)),
                dma((n_freq - 1,)), dma((n_freq - 1,)),
            ],
            compiler_params=pltpu.CompilerParams(
                collective_id=0, has_side_effects=True, vmem_limit_bytes=55150 * 1024
            ),
        )(recorded, mirror, live_counts, bins[0].T, bin_weight[0].T, taper_lo, taper_hi, gain.reshape(1, 1))

    in_specs = (
        P("freq", None, "blk", None),
        P("freq", None, None, "blk"),
        P("freq", "blk"),
        P("freq", "blk", None),
        P("freq", "blk", None),
        P("freq", "blk"),
        P("freq", "blk"),
        P("freq"),
    )
    out_specs = P("freq", None, "blk", None)
    return jax.shard_map(local, mesh=mesh, in_specs=in_specs, out_specs=out_specs, check_vma=False)
```

```python
import jax
import jax.numpy as jnp
from jax import lax
from jax.experimental import pallas as pl
from jax.experimental.pallas import tpu as pltpu
from jax.sharding import PartitionSpec as P

RAMP = 24
CUTS = 1
NY, NX, NZ, NC = 8, 4, 2, 2
MESH = pl.DeviceIdType.MESH
F32 = jnp.float32
NT = (((1,), (1,)), ((), ()))
NN = (((1,), (0,)), ((), ()))


def far_first(n):
    return sorted(range(1, n), key=lambda d: -min(d, n - d))


def make_kernel(n_freq, r_dev, src, k_dev):
    n_plane = NX * NZ
    rows = n_plane * r_dev
    n_bins = 2 * NY * n_plane
    half = NY // 2
    tail = src - 128

    def kernel(rec, mir, live, bins, wts, lo, hi, gain, out, raw, sbuf, rraw, rsend, rbuf, meta, mapt, tap, acc, asend, abuf, bsend, bbuf, esend, ebuf,
               l_sem, q_sem, word_p, word_f, s_send, s_recv, r_send, r_recv, m_send, m_recv,
               a_send, a_recv, b_send, b_recv, e_send, e_recv):
        blk = lax.axis_index("blk")
        frq = lax.axis_index("freq")
        y = blk // n_plane
        p = blk % n_plane
        x = p // NZ
        z = p % NZ

        core = frq % NC
        deep = (frq // NC) * NZ + z
        nz = (n_freq // NC) * NZ

        offsets = [(dx, dz) for dx in range(NX) for dz in range(NZ) if dx or dz]
        offsets.sort(key=lambda o: min(o[0], NX - o[0]) + o[1])

        def plane_of(dx, dz):
            return ((x + dx) % NX) * NZ + (z + dz) % NZ

        peers = [plane_of(dx, dz) for dx, dz in offsets]
        y_of = [(y + d) % NY for d in range(NY)]
        f_of = [(frq + d) % n_freq for d in range(n_freq)]

        near_y = [(y_of[d] * n_plane + p, frq) for d in (1, NY - 1)]
        near_plane = []
        for d in sorted({1 % NX, NX - 1} - {0}):
            near_plane.append((y * n_plane + ((x + d) % NX) * NZ + z, frq))
        if NZ == 2:
            near_plane.append((y * n_plane + x * NZ + 1 - z, frq))
        near_freq = []
        for d in sorted({1 % nz, nz - 1} - {0}):
            at = (deep + d) % nz
            near_freq.append((y * n_plane + x * NZ + at % NZ, (at // NZ) * NC + core))
        if NC == 2:
            near_freq.append((blk, frq - core + 1 - core))

        barrier = pltpu.get_barrier_semaphore()
        for to in near_y + near_plane + near_freq:
            pl.semaphore_signal(barrier, inc=1, device_id=to, device_id_type=MESH)

        loads = [pltpu.make_async_copy(mir.at[0, c], raw.at[c], l_sem.at[c]) for c in range(2)]
        rows_in = pltpu.make_async_copy(rec.at[0], rraw, q_sem)
        for copy in loads + [rows_in]:
            copy.start()

        on = lax.broadcasted_iota(jnp.int32, (src, k_dev), 1) < live[0, 0]
        for c in range(2):
            loads[c].wait()
            sbuf[y, c] = jnp.where(on, raw[c], jnp.zeros_like(raw[c]))

        pl.semaphore_wait(barrier, len(near_y) + len(near_plane) + len(near_freq))

        n_piece = 2 * CUTS
        piece = src // CUTS

        def ring(way, step, i, landing=False):
            owner = y - step - landing if way == 0 else y + step + landing
            part = i if way == 0 else n_piece - 1 - i
            ref = sbuf.at[(owner + NY) % NY, part // CUTS, pl.ds(part % CUTS * piece, piece), :]
            return pltpu.make_async_remote_copy(
                src_ref=ref, dst_ref=ref,
                send_sem=s_send.at[way, step * n_piece + i], recv_sem=s_recv.at[way, step * n_piece + i],
                device_id=near_y[way], device_id_type=MESH)

        def pieces(step):
            return n_piece // 2 if step == half - 1 else n_piece

        for i in range(n_piece):
            for way in range(2):
                ring(way, 0, i).start()

        def tell(word, near, i):
            for to in near:
                pl.semaphore_signal(word.at[i], inc=1, device_id=to, device_id_type=MESH)

        def heard(word, near, i):
            pl.semaphore_wait(word.at[i], len(near))

        bsend[...] = jnp.zeros_like(bsend)
        tell(word_p, near_plane, 0)
        tell(word_f, near_freq, 0)

        rows_in.wait()
        for q in range(n_plane):
            for yy in range(NY):
                at = (yy * n_plane + q) * k_dev
                rsend[q, yy] = rraw[:, :, at:at + k_dev]
        rbuf[p] = rsend[p]

        def rows_copy(i, landing=False):
            dx, dz = offsets[i]
            dst = rbuf.at[plane_of(-dx, -dz) if landing else p]
            return pltpu.make_async_remote_copy(
                src_ref=dst if landing else rsend.at[peers[i]], dst_ref=dst,
                send_sem=r_send.at[i], recv_sem=r_recv.at[i],
                device_id=(y * n_plane + peers[i], frq), device_id_type=MESH)

        def meta_copy(i):
            return pltpu.make_async_remote_copy(
                src_ref=meta.at[mine, :], dst_ref=meta.at[mine, :],
                send_sem=m_send.at[i], recv_sem=m_recv.at[i],
                device_id=(y * n_plane + peers[i], frq), device_id_type=MESH)

        def hops(i):
            return min(offsets[i][0], NX - offsets[i][0]) + offsets[i][1]

        def send_rows(far):
            for i in range(len(peers)):
                if hops(i) == far:
                    meta_copy(i).start()
                    rows_copy(i).start()


        def column(line):
            line = jnp.broadcast_to(line.astype(F32), (r_dev, r_dev))
            on = lax.broadcasted_iota(jnp.int32, (r_dev, r_dev), 0) == lax.broadcasted_iota(jnp.int32, (r_dev, r_dev), 1)
            return jnp.sum(jnp.where(on, line, 0.0), axis=1, keepdims=True)

        lane = lax.broadcasted_iota(jnp.int32, (r_dev, 128), 1)
        table = jnp.zeros((r_dev, 128), F32)
        for i, line in enumerate([bins[0:1], bins[1:2], wts[0:1], wts[1:2], lo[...], hi[...]]):
            table = jnp.where(lane == i, column(line), table)
        mine = pl.ds(pl.multiple_of(p * r_dev, r_dev), r_dev)
        meta[mine, :] = table

        send_rows(1)

        def pass_on(step):
            for i in range(pieces(step)):
                for way in range(2):
                    ring(way, step, i, landing=True).wait_recv()
                    if step + 1 < half and i < pieces(step + 1):
                        ring(way, step + 1, i).start()

        def from_peer(i):
            dx, dz = offsets[i]
            q = plane_of(-dx, -dz)
            rows_q = pl.ds(pl.multiple_of(q * r_dev, r_dev), r_dev)
            pltpu.make_async_remote_copy(
                src_ref=meta.at[rows_q, :], dst_ref=meta.at[rows_q, :],
                send_sem=m_send.at[i], recv_sem=m_recv.at[i],
                device_id=(y * n_plane + peers[i], frq), device_id_type=MESH).wait_recv()

        heard(word_p, near_plane, 0)
        tell(word_p, near_plane, 1)
        send_rows(2)
        pass_on(0)
        if half > 2:
            pass_on(1)
        heard(word_p, near_plane, 1)
        send_rows(3)
        heard(word_f, near_freq, 0)
        tell(word_f, near_freq, 1)
        for step in range(2, half - 1):
            pass_on(step)
        heard(word_f, near_freq, 1)
        tell(word_f, near_freq, 2)

        for i in range(len(peers)):
            from_peer(i)
        info = meta[...]
        place = lax.broadcasted_iota(jnp.int32, (rows, n_bins), 1)
        per = 2 * NY
        named = (place % per // 2) * (2 * n_plane) + (place // per) * 2 + place % 2
        named = named.astype(F32)
        spread = jnp.where(info[:, 0:1] == named, info[:, 2:3], 0.0) + jnp.where(info[:, 1:2] == named, info[:, 3:4], 0.0)
        mapt[...] = spread.T
        at = lax.broadcasted_iota(jnp.int32, (rows, src), 1).astype(F32)
        rise = jnp.clip((at - info[:, 4:5] + 1.0) / RAMP, 0.0, 1.0)
        fall = jnp.clip((info[:, 5:6] - at) / RAMP, 0.0, 1.0)
        tap[...] = rise * fall


        for i in range(len(peers)):
            rows_copy(i, landing=True).wait_recv()

        def product(blocks):
            at = [y_of[d % NY] for d in blocks]
            left = jnp.concatenate([rbuf[:, yy].reshape(2 * rows, k_dev) for yy in at], axis=1)
            return [lax.dot_general(left, jnp.concatenate([sbuf[yy, c] for yy in at], axis=1), NT, preferred_element_type=F32)
                    for c in range(2)]

        for c, part in enumerate(product([d for d in range(NY) if d != half])):
            acc[c] = part
        pass_on(half - 1)
        for c, part in enumerate(product([half])):
            acc[c] += part

        def of(c, part):
            return acc[c].reshape(n_plane, 2, r_dev, src)[:, part].reshape(rows, src)

        binned = []
        for c in range(2):
            if c == 0:
                value = of(0, 0) - of(1, 1)
            else:
                value = of(1, 0) + of(0, 1)
            value = value * tap[...]
            top = value.astype(jnp.bfloat16)
            low = (value - top.astype(F32)).astype(jnp.bfloat16)
            weight_top = mapt[...].astype(jnp.bfloat16)
            weight_low = (mapt[...] - weight_top.astype(F32)).astype(jnp.bfloat16)
            binned.append(sum(lax.dot_general(m, v, NN, preferred_element_type=F32)
                              for m, v in ((weight_top, low), (weight_low, top), (weight_top, top))))
        asend[:, 0:128] = binned[0][:, 0:128]
        asend[:, 128:256] = binned[1][:, 0:128]
        asend[:, 256:256 + tail] = binned[0][:, 128:src]
        asend[:, 256 + tail:256 + 2 * tail] = binned[1][:, 128:src]

        def a_copy(i):
            to = pl.ds(pl.multiple_of(peers[i] * per, per), per)
            return pltpu.make_async_remote_copy(
                src_ref=asend.at[to, :], dst_ref=abuf.at[i],
                send_sem=a_send.at[i], recv_sem=a_recv.at[i],
                device_id=(y * n_plane + peers[i], frq), device_id_type=MESH)

        for i in reversed(range(len(peers))):
            a_copy(i).start()
        heard(word_f, near_freq, 2)
        tell(word_f, near_freq, 3)
        total = asend[pl.ds(pl.multiple_of(p * per, per), per), :]
        for i in range(len(peers)):
            a_copy(i).wait_recv()
            total = total + abuf[i]

        for d in range(NY):
            for k in range(3):
                bsend[d, 2 * k:2 * k + 2, :] = total[2 * d:2 * d + 2, 128 * k:128 * k + 128]

        def b_copy(d):
            return pltpu.make_async_remote_copy(
                src_ref=bsend.at[y_of[d]], dst_ref=bbuf.at[d - 1],
                send_sem=b_send.at[d - 1], recv_sem=b_recv.at[d - 1],
                device_id=(y_of[d] * n_plane + p, frq), device_id_type=MESH)

        for d in far_first(NY):
            b_copy(d).start()
        tile = bsend[y]
        for d in range(1, NY):
            b_copy(d).wait_recv()
            tile = tile + bbuf[d - 1]
        scaled = tile * gain[0]
        square = scaled * scaled
        esend[...] = square

        def e_copy(d):
            return pltpu.make_async_remote_copy(
                src_ref=esend, dst_ref=ebuf.at[d - 1],
                send_sem=e_send.at[d - 1], recv_sem=e_recv.at[d - 1],
                device_id=(blk, f_of[d]), device_id_type=MESH)

        heard(word_f, near_freq, 3)
        for d in far_first(n_freq):
            e_copy(d).start()
        for step in range(half):
            for i in range(pieces(step)):
                for way in range(2):
                    ring(way, step, i).wait_send()
        for i in range(len(peers)):
            rows_copy(i).wait_send()
            meta_copy(i).wait_send()
            a_copy(i).wait_send()
        for d in range(1, NY):
            b_copy(d).wait_send()
        for d in range(1, n_freq):
            e_copy(d).wait_recv()
            square = square + ebuf[d - 1]
        for d in range(1, n_freq):
            e_copy(d).wait_send()
        energy = jnp.sum(square[0:2] + square[2:4] + square[4:6], axis=1, keepdims=True)
        norm = jnp.sqrt(energy / (n_freq * 2 * src) + 1e-06)
        for c in range(2):
            out[0, c, :, 0:128] = scaled[2 * c:2 * c + 2] / norm
            out[0, c, :, 128:src] = scaled[4:6, c * tail:(c + 1) * tail] / norm

    return kernel


def solution(mesh):
    n_freq = mesh.shape["freq"]

    def local(recorded, mirror, live_counts, bins, bin_weight, taper_lo, taper_hi, gain):
        r_dev = recorded.shape[2]
        src, k_dev = mirror.shape[2], mirror.shape[3]
        n_plane = NX * NZ
        rows, per, n_peer, half = n_plane * r_dev, 2 * NY, n_plane - 1, NY // 2
        hbm, vmem, smem = (pl.BlockSpec(memory_space=m) for m in (pltpu.HBM, pltpu.VMEM, pltpu.SMEM))
        dma = pltpu.SemaphoreType.DMA
        bf16 = jnp.bfloat16
        return pl.pallas_call(
            make_kernel(n_freq, r_dev, src, k_dev),
            out_shape=jax.ShapeDtypeStruct((1, 2, 2, src), F32),
            in_specs=[hbm, hbm, smem, vmem, vmem, vmem, vmem, smem],
            out_specs=vmem,
            scratch_shapes=[
                pltpu.VMEM((2, src, k_dev), bf16),
                pltpu.VMEM((NY, 2, src, k_dev), bf16),
                pltpu.VMEM((2, r_dev, NY * n_plane * k_dev), bf16),
                pltpu.VMEM((n_plane, NY, 2, r_dev, k_dev), bf16),
                pltpu.VMEM((n_plane, NY, 2, r_dev, k_dev), bf16),
                pltpu.VMEM((rows, 128), F32),
                pltpu.VMEM((2 * NY * n_plane, rows), F32),
                pltpu.VMEM((rows, src), F32),
                pltpu.VMEM((2, 2 * rows, src), F32),
                pltpu.VMEM((per * n_plane, 2 * src), F32),
                pltpu.VMEM((n_peer, per, 2 * src), F32),
                pltpu.VMEM((NY, 8, 128), F32),
                pltpu.VMEM((NY - 1, 8, 128), F32),
                pltpu.VMEM((8, 128), F32),
                pltpu.VMEM((n_freq - 1, 8, 128), F32),
                dma((2,)), dma, pltpu.SemaphoreType.REGULAR((2,)), pltpu.SemaphoreType.REGULAR((4,)),
                dma((2, 2 * CUTS * half)), dma((2, 2 * CUTS * half)),
                dma((n_peer,)), dma((n_peer,)),
                dma((n_peer,)), dma((n_peer,)),
                dma((n_peer,)), dma((n_peer,)),
                dma((NY - 1,)), dma((NY - 1,)),
                dma((n_freq - 1,)), dma((n_freq - 1,)),
            ],
            compiler_params=pltpu.CompilerParams(
                collective_id=0, has_side_effects=True, vmem_limit_bytes=55150 * 1024
            ),
        )(recorded, mirror, live_counts, bins[0].T, bin_weight[0].T, taper_lo, taper_hi, gain)

    in_specs = (
        P("freq", None, "blk", None),
        P("freq", None, None, "blk"),
        P("freq", "blk"),
        P("freq", "blk", None),
        P("freq", "blk", None),
        P("freq", "blk"),
        P("freq", "blk"),
        P("freq"),
    )
    out_specs = P("freq", None, "blk", None)
    return jax.shard_map(local, mesh=mesh, in_specs=in_specs, out_specs=out_specs, check_vma=False)
```

```python
import jax
import jax.numpy as jnp
from jax import lax
from jax.experimental import pallas as pl
from jax.experimental.pallas import tpu as pltpu
from jax.sharding import PartitionSpec as P

RAMP = 24
CUTS = 2
NY, NX, NZ, NC = 8, 4, 2, 2
MESH = pl.DeviceIdType.MESH
F32 = jnp.float32
NT = (((1,), (1,)), ((), ()))
NN = (((1,), (0,)), ((), ()))


def far_first(n):
    return sorted(range(1, n), key=lambda d: -min(d, n - d))


def make_kernel(n_freq, r_dev, src, k_dev):
    n_plane = NX * NZ
    rows = n_plane * r_dev
    n_bins = 2 * NY * n_plane
    half = NY // 2
    tail = src - 128

    def kernel(rec, mir, live, bins, wts, lo, hi, gain, out, raw, sbuf, rraw, rsend, rbuf, meta, mapt, tap, acc, asend, abuf, bsend, bbuf, esend, ebuf,
               l_sem, q_sem, word_p, word_f, s_send, s_recv, r_send, r_recv, m_send, m_recv,
               a_send, a_recv, b_send, b_recv, e_send, e_recv):
        blk = lax.axis_index("blk")
        frq = lax.axis_index("freq")
        y = blk // n_plane
        p = blk % n_plane
        x = p // NZ
        z = p % NZ

        core = frq % NC
        deep = (frq // NC) * NZ + z
        nz = (n_freq // NC) * NZ

        offsets = [(dx, dz) for dx in range(NX) for dz in range(NZ) if dx or dz]
        offsets.sort(key=lambda o: min(o[0], NX - o[0]) + o[1])

        def plane_of(dx, dz):
            return ((x + dx) % NX) * NZ + (z + dz) % NZ

        peers = [plane_of(dx, dz) for dx, dz in offsets]
        y_of = [(y + d) % NY for d in range(NY)]
        f_of = [(frq + d) % n_freq for d in range(n_freq)]

        near_y = [(y_of[d] * n_plane + p, frq) for d in (1, NY - 1)]
        near_plane = []
        for d in sorted({1 % NX, NX - 1} - {0}):
            near_plane.append((y * n_plane + ((x + d) % NX) * NZ + z, frq))
        if NZ == 2:
            near_plane.append((y * n_plane + x * NZ + 1 - z, frq))
        near_freq = []
        for d in sorted({1 % nz, nz - 1} - {0}):
            at = (deep + d) % nz
            near_freq.append((y * n_plane + x * NZ + at % NZ, (at // NZ) * NC + core))
        if NC == 2:
            near_freq.append((blk, frq - core + 1 - core))

        barrier = pltpu.get_barrier_semaphore()
        for to in near_y + near_plane + near_freq:
            pl.semaphore_signal(barrier, inc=1, device_id=to, device_id_type=MESH)

        loads = [pltpu.make_async_copy(mir.at[0, c], raw.at[c], l_sem.at[c]) for c in range(2)]
        rows_in = pltpu.make_async_copy(rec.at[0], rraw, q_sem)
        for copy in loads + [rows_in]:
            copy.start()

        on = lax.broadcasted_iota(jnp.int32, (src, k_dev), 1) < live[0, 0]
        for c in range(2):
            loads[c].wait()
            sbuf[y, c] = jnp.where(on, raw[c], jnp.zeros_like(raw[c]))

        pl.semaphore_wait(barrier, len(near_y) + len(near_plane) + len(near_freq))

        n_piece = 2 * CUTS
        piece = src // CUTS

        def ring(way, step, i, landing=False):
            owner = y - step - landing if way == 0 else y + step + landing
            part = i if way == 0 else n_piece - 1 - i
            ref = sbuf.at[(owner + NY) % NY, part // CUTS, pl.ds(part % CUTS * piece, piece), :]
            return pltpu.make_async_remote_copy(
                src_ref=ref, dst_ref=ref,
                send_sem=s_send.at[way, step * n_piece + i], recv_sem=s_recv.at[way, step * n_piece + i],
                device_id=near_y[way], device_id_type=MESH)

        def pieces(step):
            return n_piece // 2 if step == half - 1 else n_piece

        for i in range(n_piece):
            for way in range(2):
                ring(way, 0, i).start()

        def tell(word, near, i):
            for to in near:
                pl.semaphore_signal(word.at[i], inc=1, device_id=to, device_id_type=MESH)

        def heard(word, near, i):
            pl.semaphore_wait(word.at[i], len(near))

        bsend[...] = jnp.zeros_like(bsend)
        tell(word_p, near_plane, 0)
        tell(word_f, near_freq, 0)

        rows_in.wait()
        for q in range(n_plane):
            for yy in range(NY):
                at = (yy * n_plane + q) * k_dev
                rsend[q, yy] = rraw[:, :, at:at + k_dev]
        rbuf[p] = rsend[p]

        def rows_copy(i, landing=False):
            dx, dz = offsets[i]
            dst = rbuf.at[plane_of(-dx, -dz) if landing else p]
            return pltpu.make_async_remote_copy(
                src_ref=dst if landing else rsend.at[peers[i]], dst_ref=dst,
                send_sem=r_send.at[i], recv_sem=r_recv.at[i],
                device_id=(y * n_plane + peers[i], frq), device_id_type=MESH)

        def meta_copy(i):
            return pltpu.make_async_remote_copy(
                src_ref=meta.at[mine, :], dst_ref=meta.at[mine, :],
                send_sem=m_send.at[i], recv_sem=m_recv.at[i],
                device_id=(y * n_plane + peers[i], frq), device_id_type=MESH)

        def hops(i):
            return min(offsets[i][0], NX - offsets[i][0]) + offsets[i][1]

        def send_rows(far):
            for i in range(len(peers)):
                if hops(i) == far:
                    meta_copy(i).start()
                    rows_copy(i).start()


        def column(line):
            line = jnp.broadcast_to(line.astype(F32), (r_dev, r_dev))
            on = lax.broadcasted_iota(jnp.int32, (r_dev, r_dev), 0) == lax.broadcasted_iota(jnp.int32, (r_dev, r_dev), 1)
            return jnp.sum(jnp.where(on, line, 0.0), axis=1, keepdims=True)

        lane = lax.broadcasted_iota(jnp.int32, (r_dev, 128), 1)
        table = jnp.zeros((r_dev, 128), F32)
        for i, line in enumerate([bins[0:1], bins[1:2], wts[0:1], wts[1:2], lo[...], hi[...]]):
            table = jnp.where(lane == i, column(line), table)
        mine = pl.ds(pl.multiple_of(p * r_dev, r_dev), r_dev)
        meta[mine, :] = table

        send_rows(1)

        def pass_on(step):
            for i in range(pieces(step)):
                for way in range(2):
                    ring(way, step, i, landing=True).wait_recv()
                    if step + 1 < half and i < pieces(step + 1):
                        ring(way, step + 1, i).start()

        def from_peer(i):
            dx, dz = offsets[i]
            q = plane_of(-dx, -dz)
            rows_q = pl.ds(pl.multiple_of(q * r_dev, r_dev), r_dev)
            pltpu.make_async_remote_copy(
                src_ref=meta.at[rows_q, :], dst_ref=meta.at[rows_q, :],
                send_sem=m_send.at[i], recv_sem=m_recv.at[i],
                device_id=(y * n_plane + peers[i], frq), device_id_type=MESH).wait_recv()

        heard(word_p, near_plane, 0)
        tell(word_p, near_plane, 1)
        send_rows(2)
        pass_on(0)
        if half > 2:
            pass_on(1)
        heard(word_p, near_plane, 1)
        send_rows(3)
        heard(word_f, near_freq, 0)
        tell(word_f, near_freq, 1)
        for step in range(2, half - 1):
            pass_on(step)
        heard(word_f, near_freq, 1)
        tell(word_f, near_freq, 2)

        for i in range(len(peers)):
            from_peer(i)
        info = meta[...]
        place = lax.broadcasted_iota(jnp.int32, (rows, n_bins), 1)
        per = 2 * NY
        named = (place % per // 2) * (2 * n_plane) + (place // per) * 2 + place % 2
        named = named.astype(F32)
        spread = jnp.where(info[:, 0:1] == named, info[:, 2:3], 0.0) + jnp.where(info[:, 1:2] == named, info[:, 3:4], 0.0)
        mapt[...] = spread.T
        at = lax.broadcasted_iota(jnp.int32, (rows, src), 1).astype(F32)
        rise = jnp.clip((at - info[:, 4:5] + 1.0) / RAMP, 0.0, 1.0)
        fall = jnp.clip((info[:, 5:6] - at) / RAMP, 0.0, 1.0)
        tap[...] = rise * fall


        for i in range(len(peers)):
            rows_copy(i, landing=True).wait_recv()

        def product(blocks):
            at = [y_of[d % NY] for d in blocks]
            left = jnp.concatenate([rbuf[:, yy].reshape(2 * rows, k_dev) for yy in at], axis=1)
            return [lax.dot_general(left, jnp.concatenate([sbuf[yy, c] for yy in at], axis=1), NT, preferred_element_type=F32)
                    for c in range(2)]

        for c, part in enumerate(product([d for d in range(NY) if d != half])):
            acc[c] = part
        pass_on(half - 1)
        for c, part in enumerate(product([half])):
            acc[c] += part

        def of(c, part):
            return acc[c].reshape(n_plane, 2, r_dev, src)[:, part].reshape(rows, src)

        binned = []
        for c in range(2):
            if c == 0:
                value = of(0, 0) - of(1, 1)
            else:
                value = of(1, 0) + of(0, 1)
            value = value * tap[...]
            top = value.astype(jnp.bfloat16)
            low = (value - top.astype(F32)).astype(jnp.bfloat16)
            weight_top = mapt[...].astype(jnp.bfloat16)
            weight_low = (mapt[...] - weight_top.astype(F32)).astype(jnp.bfloat16)
            binned.append(sum(lax.dot_general(m, v, NN, preferred_element_type=F32)
                              for m, v in ((weight_top, low), (weight_low, top), (weight_top, top))))
        asend[:, 0:128] = binned[0][:, 0:128]
        asend[:, 128:256] = binned[1][:, 0:128]
        asend[:, 256:256 + tail] = binned[0][:, 128:src]
        asend[:, 256 + tail:256 + 2 * tail] = binned[1][:, 128:src]

        def a_copy(i):
            to = pl.ds(pl.multiple_of(peers[i] * per, per), per)
            return pltpu.make_async_remote_copy(
                src_ref=asend.at[to, :], dst_ref=abuf.at[i],
                send_sem=a_send.at[i], recv_sem=a_recv.at[i],
                device_id=(y * n_plane + peers[i], frq), device_id_type=MESH)

        for i in reversed(range(len(peers))):
            a_copy(i).start()
        heard(word_f, near_freq, 2)
        tell(word_f, near_freq, 3)
        total = asend[pl.ds(pl.multiple_of(p * per, per), per), :]
        for i in range(len(peers)):
            a_copy(i).wait_recv()
            total = total + abuf[i]

        for d in range(NY):
            for k in range(3):
                bsend[d, 2 * k:2 * k + 2, :] = total[2 * d:2 * d + 2, 128 * k:128 * k + 128]

        def b_copy(d):
            return pltpu.make_async_remote_copy(
                src_ref=bsend.at[y_of[d]], dst_ref=bbuf.at[d - 1],
                send_sem=b_send.at[d - 1], recv_sem=b_recv.at[d - 1],
                device_id=(y_of[d] * n_plane + p, frq), device_id_type=MESH)

        for d in far_first(NY):
            b_copy(d).start()
        tile = bsend[y]
        for d in range(1, NY):
            b_copy(d).wait_recv()
            tile = tile + bbuf[d - 1]
        scaled = tile * gain[0]
        square = scaled * scaled
        esend[...] = square

        def e_copy(d):
            return pltpu.make_async_remote_copy(
                src_ref=esend, dst_ref=ebuf.at[d - 1],
                send_sem=e_send.at[d - 1], recv_sem=e_recv.at[d - 1],
                device_id=(blk, f_of[d]), device_id_type=MESH)

        heard(word_f, near_freq, 3)
        for d in far_first(n_freq):
            e_copy(d).start()
        for step in range(half):
            for i in range(pieces(step)):
                for way in range(2):
                    ring(way, step, i).wait_send()
        for i in range(len(peers)):
            rows_copy(i).wait_send()
            meta_copy(i).wait_send()
            a_copy(i).wait_send()
        for d in range(1, NY):
            b_copy(d).wait_send()
        for d in range(1, n_freq):
            e_copy(d).wait_recv()
            square = square + ebuf[d - 1]
        for d in range(1, n_freq):
            e_copy(d).wait_send()
        energy = jnp.sum(square[0:2] + square[2:4] + square[4:6], axis=1, keepdims=True)
        norm = jnp.sqrt(energy / (n_freq * 2 * src) + 1e-06)
        for c in range(2):
            out[0, c, :, 0:128] = scaled[2 * c:2 * c + 2] / norm
            out[0, c, :, 128:src] = scaled[4:6, c * tail:(c + 1) * tail] / norm

    return kernel


def solution(mesh):
    n_freq = mesh.shape["freq"]

    def local(recorded, mirror, live_counts, bins, bin_weight, taper_lo, taper_hi, gain):
        r_dev = recorded.shape[2]
        src, k_dev = mirror.shape[2], mirror.shape[3]
        n_plane = NX * NZ
        rows, per, n_peer, half = n_plane * r_dev, 2 * NY, n_plane - 1, NY // 2
        hbm, vmem, smem = (pl.BlockSpec(memory_space=m) for m in (pltpu.HBM, pltpu.VMEM, pltpu.SMEM))
        dma = pltpu.SemaphoreType.DMA
        bf16 = jnp.bfloat16
        return pl.pallas_call(
            make_kernel(n_freq, r_dev, src, k_dev),
            out_shape=jax.ShapeDtypeStruct((1, 2, 2, src), F32),
            in_specs=[hbm, hbm, smem, vmem, vmem, vmem, vmem, smem],
            out_specs=vmem,
            scratch_shapes=[
                pltpu.VMEM((2, src, k_dev), bf16),
                pltpu.VMEM((NY, 2, src, k_dev), bf16),
                pltpu.VMEM((2, r_dev, NY * n_plane * k_dev), bf16),
                pltpu.VMEM((n_plane, NY, 2, r_dev, k_dev), bf16),
                pltpu.VMEM((n_plane, NY, 2, r_dev, k_dev), bf16),
                pltpu.VMEM((rows, 128), F32),
                pltpu.VMEM((2 * NY * n_plane, rows), F32),
                pltpu.VMEM((rows, src), F32),
                pltpu.VMEM((2, 2 * rows, src), F32),
                pltpu.VMEM((per * n_plane, 2 * src), F32),
                pltpu.VMEM((n_peer, per, 2 * src), F32),
                pltpu.VMEM((NY, 8, 128), F32),
                pltpu.VMEM((NY - 1, 8, 128), F32),
                pltpu.VMEM((8, 128), F32),
                pltpu.VMEM((n_freq - 1, 8, 128), F32),
                dma((2,)), dma, pltpu.SemaphoreType.REGULAR((2,)), pltpu.SemaphoreType.REGULAR((4,)),
                dma((2, 2 * CUTS * half)), dma((2, 2 * CUTS * half)),
                dma((n_peer,)), dma((n_peer,)),
                dma((n_peer,)), dma((n_peer,)),
                dma((n_peer,)), dma((n_peer,)),
                dma((NY - 1,)), dma((NY - 1,)),
                dma((n_freq - 1,)), dma((n_freq - 1,)),
            ],
            compiler_params=pltpu.CompilerParams(
                collective_id=0, has_side_effects=True, vmem_limit_bytes=55150 * 1024
            ),
        )(recorded, mirror, live_counts, bins[0].T, bin_weight[0].T, taper_lo, taper_hi, gain)

    in_specs = (
        P("freq", None, "blk", None),
        P("freq", None, None, "blk"),
        P("freq", "blk"),
        P("freq", "blk", None),
        P("freq", "blk", None),
        P("freq", "blk"),
        P("freq", "blk"),
        P("freq"),
    )
    out_specs = P("freq", None, "blk", None)
    return jax.shard_map(local, mesh=mesh, in_specs=in_specs, out_specs=out_specs, check_vma=False)
```
